256 devices in a mesh: rows: 16 (over y_hi, z), cols: 4 (over y_lo, core), rep: 4 (over x).
Axes of the slice: x: 4, y: 4 (y_hi: 2, y_lo: 2; y = y_hi * 2 + y_lo), z: 8, core: 2. Of those that a mesh axis runs over, the one named last changes fastest.
Arguments:
- image: bfloat16 [4, 256, 128, 1024], P('rep', 'rows', 'cols'), may hold values from -6 to 6
- cotangent: bfloat16 [4, 256, 128, 1024], P('rep', 'rows', 'cols'), may hold values from -6 to 6
- gain: float32 [1024], replicated, may hold values from 0.5 to 1.5
- w_qkv: bfloat16 [1024, 1536], replicated, may hold values from -0.1875 to 0.1875
- w_out: bfloat16 [512, 1024], replicated, may hold values from -0.25 to 0.25
- bias_table: float32 [8, 15, 15], replicated, may hold values from -4 to 300
Outputs:
- output: bfloat16 [4, 256, 128, 1024], P('rep', 'rows', 'cols')
- grad_image: bfloat16 [4, 256, 128, 1024], P('rep', 'rows', 'cols')
- grad_qkv: float32 [1024, 1536], P(('rows', 'cols', 'rep'))
- grad_out: float32 [512, 1024], P(None, ('rows', 'cols', 'rep'))
- grad_gain: float32 [1024], P(('rows', 'cols', 'rep'))
The draws below stay inside these ranges and needn't reach their ends.
All inputs are finite; a program needn't handle non-finite values.
Results may differ from the reference program's by a relative error of at most 0.0091.
Values may be sent and summed in bfloat16 or wider, within the bound.
A program may use at most 128 MiB of HBM per device.

```python
import jax
import jax.numpy as jnp
import numpy as np
from jax import lax

D = 1024
HEADS = 8
WIN = 8
SHIFT = 4
HD = 512
H = 256
W = 128
BATCH = 4
TOKENS = 131072


def draw_bias_table(key, part):
    key = jax.random.fold_in(key, 11)
    table_side = 2 * WIN - 1
    normal_part = jnp.clip(jax.random.normal(key, (HEADS, table_side * table_side), jnp.float32), -4.0, 4.0)
    return normal_part.reshape(HEADS, table_side, table_side)


def with_spikes(values, key, source, target, parts, factor):
    owner, partner = [(jnp.arange(values.shape[dim]) // (values.shape[dim] // parts)).reshape([-1 if axis == dim else 1 for axis in range(values.ndim)]) for dim in (source, target)]
    chosen = jax.random.permutation(key, parts)[partner]
    strong = (owner == chosen) | (owner == (partner + parts // 2) % parts)
    return jnp.where(strong, factor * values, values)


def block_levels(stream_key, extent, split, least, largest):
    factor_of, own = 1.0, jax.random.fold_in(stream_key, 6)
    for dim, blocks in split:
        steps = jnp.exp(jax.random.uniform(jax.random.fold_in(own, dim), (blocks,), jnp.float32, least / len(split), largest / len(split)))
        factor_of = factor_of * jnp.repeat(steps, extent[dim] // blocks).reshape([-1 if axis == dim else 1 for axis in range(len(extent))])
    return factor_of


def centred(rng, extent, deviation, reach, split=(), kind=jnp.bfloat16):
    values = deviation * jax.random.normal(rng, extent, jnp.float32)
    if split:
        values = values * block_levels(rng, extent, split, -0.22, 0.18)
    return jnp.clip(values, -reach, reach).astype(kind)


def noise_with(own_key, extent, spread, limit, cuts, heavy, held_as=jnp.bfloat16):
    entries = spread * jax.random.normal(own_key, extent, jnp.float32)
    if cuts:
        entries = entries * block_levels(own_key, extent, cuts, -0.22, 0.18)
    return jnp.clip(with_spikes(entries, jax.random.fold_in(own_key, 3), *heavy), -limit, limit).astype(held_as)


def setup_inputs(seed: int = 0) -> dict:
    seeds = jax.random.split(jax.random.key(seed), 7)
    image = noise_with(seeds[0], (BATCH, H, W, D), 1.0, 6.0, ((0, 4), (1, 16), (2, 4)), (1, 3, 16, 2.0))
    cotangent = noise_with(seeds[1], (BATCH, H, W, D), 1.0, 6.0, ((0, 4), (1, 16), (2, 4)), (2, 3, 4, 2.0))
    gain = jnp.clip(1.0 + 0.1 * jax.random.normal(seeds[2], (D,), jnp.float32), 0.5, 1.5)
    w_qkv = centred(seeds[3], (D, 3 * HD), D ** -0.5, 0.1875)
    w_out = centred(seeds[4], (HD, D), HD ** -0.5, 0.25)
    bias_table = draw_bias_table(jax.random.fold_in(seeds[6], 71), 0)
    return dict(image=image, cotangent=cotangent, gain=gain, w_qkv=w_qkv, w_out=w_out, bias_table=bias_table)


EPS = 1e-06

def offset_tables(window):
    position = np.arange(window * window)
    row_pos = position // window
    col_pos = position % window
    row_offset = row_pos[:, None] - row_pos[None, :] + window - 1
    col_offset = col_pos[:, None] - col_pos[None, :] + window - 1
    return (row_offset, col_offset)

def to_windows(tokens, window):
    rows_n, cols_n, chans = tokens.shape
    blocks = tokens.reshape(rows_n // window, window, cols_n // window, window, chans)
    return blocks.transpose(0, 2, 1, 3, 4).reshape(-1, window * window, chans)

def from_windows(blocks, rows_n, cols_n, window):
    chans = blocks.shape[-1]
    grid = blocks.reshape(rows_n // window, cols_n // window, window, window, chans)
    return grid.transpose(0, 2, 1, 3, 4).reshape(rows_n, cols_n, chans)

def window_block(shifted, grad_shifted, gain, w_qkv, w_out, bias_table):
    f32 = jnp.float32
    bf16 = jnp.bfloat16
    rows_n, cols_n, features = shifted.shape
    head_count = bias_table.shape[0]
    window = (bias_table.shape[1] + 1) // 2
    all_heads = w_out.shape[0]
    head_size = all_heads // head_count
    score_scale = head_size ** (-0.5)
    flat_rows = shifted.reshape(rows_n * cols_n, features).astype(f32)
    inverse = lax.rsqrt(lax.optimization_barrier(jnp.mean(flat_rows * flat_rows, axis=1, keepdims=True)) + EPS)
    unit_rows = flat_rows * inverse
    normed = (unit_rows * gain).astype(bf16)
    projected = jnp.dot(normed, w_qkv, preferred_element_type=f32).astype(bf16)
    win_proj = to_windows(projected.reshape(rows_n, cols_n, 3 * all_heads), window)
    count_win = win_proj.shape[0]
    win_proj = win_proj.reshape(count_win, window * window, 3, head_count, head_size)
    queries = win_proj[:, :, 0].astype(f32)
    keys_win = win_proj[:, :, 1].astype(f32)
    values_win = win_proj[:, :, 2].astype(f32)
    row_offset, col_offset = offset_tables(window)
    bias = bias_table[:, row_offset, col_offset]
    scores = jnp.einsum('nqhe,nkhe->nhqk', queries, keys_win) * score_scale + bias[None]
    peak = lax.optimization_barrier(jnp.max(scores, axis=-1, keepdims=True))
    expo = jnp.exp(scores - peak)
    softmax_f = expo / lax.optimization_barrier(jnp.sum(expo, axis=-1, keepdims=True))
    softmax_b = softmax_f.astype(bf16)
    heads_win = jnp.einsum('nhqk,nkhe->nqhe', softmax_b.astype(f32), values_win).astype(bf16)
    heads_out = from_windows(heads_win.reshape(count_win, window * window, all_heads), rows_n, cols_n, window)
    heads_out = heads_out.reshape(rows_n * cols_n, all_heads)
    attention = jnp.dot(heads_out, w_out, preferred_element_type=f32).astype(bf16)
    upstream = grad_shifted.reshape(rows_n * cols_n, features)
    part_out = jnp.dot(heads_out.T, upstream, preferred_element_type=f32)
    grad_heads = jnp.dot(upstream, w_out.T, preferred_element_type=f32).astype(bf16)
    grad_win = to_windows(grad_heads.reshape(rows_n, cols_n, all_heads), window)
    grad_win = grad_win.reshape(count_win, window * window, head_count, head_size).astype(f32)
    grad_probs = jnp.einsum('nqhe,nkhe->nhqk', grad_win, values_win)
    grad_values = jnp.einsum('nhqk,nqhe->nkhe', softmax_b.astype(f32), grad_win).astype(bf16)
    inner = lax.optimization_barrier(jnp.sum(grad_probs * softmax_f, axis=-1, keepdims=True))
    grad_scores = (softmax_f * (grad_probs - inner) * score_scale).astype(bf16).astype(f32)
    grad_queries = jnp.einsum('nhqk,nkhe->nqhe', grad_scores, keys_win).astype(bf16)
    grad_keys = jnp.einsum('nhqk,nqhe->nkhe', grad_scores, queries).astype(bf16)
    grad_projected = jnp.stack([grad_queries, grad_keys, grad_values], axis=2)
    grad_projected = grad_projected.reshape(count_win, window * window, 3 * all_heads)
    grad_projected = from_windows(grad_projected, rows_n, cols_n, window).reshape(rows_n * cols_n, 3 * all_heads)
    part_qkv = jnp.dot(normed.T, grad_projected, preferred_element_type=f32)
    grad_normed = jnp.dot(grad_projected, w_qkv.T, preferred_element_type=f32)
    part_gain = lax.optimization_barrier(jnp.sum(grad_normed * unit_rows, axis=0))
    grad_unit = grad_normed * gain
    grad_tokens = inverse * (grad_unit - unit_rows * lax.optimization_barrier(jnp.mean(grad_unit * unit_rows, axis=1, keepdims=True)))
    grad_tokens = grad_tokens.astype(bf16)
    return (attention.reshape(rows_n, cols_n, features), grad_tokens.reshape(rows_n, cols_n, features), part_qkv, part_out, part_gain)

def reference(image, cotangent, gain, w_qkv, w_out, bias_table):
    f32 = jnp.float32

    def per_image(paired):
        latent, grad_in = paired
        shifted = jnp.roll(latent, (-SHIFT, -SHIFT), (0, 1))
        grad_shifted = jnp.roll(grad_in, (-SHIFT, -SHIFT), (0, 1))
        attention, grad_tokens, part_qkv, part_out, part_gain = window_block(shifted, grad_shifted, gain, w_qkv, w_out, bias_table)
        result = (latent.astype(f32) + jnp.roll(attention, (SHIFT, SHIFT), (0, 1)).astype(f32)).astype(jnp.bfloat16)
        grad_result = (grad_in.astype(f32) + jnp.roll(grad_tokens, (SHIFT, SHIFT), (0, 1)).astype(f32)).astype(jnp.bfloat16)
        return (result, grad_result, part_qkv, part_out, part_gain)
    outputs, grad_image, part_qkv, part_out, part_gain = lax.map(per_image, (image, cotangent))
    factor = 1.0 / float(np.sqrt(TOKENS))
    return (outputs, grad_image, lax.optimization_barrier(jnp.sum(part_qkv, axis=0)) * factor, lax.optimization_barrier(jnp.sum(part_out, axis=0)) * factor, lax.optimization_barrier(jnp.sum(part_gain, axis=0)) * factor)
```

```python
import functools

import jax
import jax.numpy as jnp
import numpy as np
from jax import lax
from jax.experimental import pallas as pl
from jax.experimental.pallas import tpu as pltpu
from jax.sharding import PartitionSpec as P

MESH = pl.DeviceIdType.MESH

SHIFT = 4


EPS = 1e-06


def passed_along(value, axis, steps):
    count = lax.axis_size(axis)
    pairs = [(source, (source + steps) % count) for source in range(count)]
    return lax.ppermute(value, axis, pairs)


def offset_tables(window):
    position = np.arange(window * window)
    row_pos = position // window
    col_pos = position % window
    row_offset = row_pos[:, None] - row_pos[None, :] + window - 1
    col_offset = col_pos[:, None] - col_pos[None, :] + window - 1
    return (row_offset, col_offset)


def to_windows(tokens, window):
    rows_n, cols_n, chans = tokens.shape
    blocks = tokens.reshape(rows_n // window, window, cols_n // window, window, chans)
    return blocks.transpose(0, 2, 1, 3, 4).reshape(-1, window * window, chans)


def from_windows(blocks, rows_n, cols_n, window):
    chans = blocks.shape[-1]
    grid = blocks.reshape(rows_n // window, cols_n // window, window, window, chans)
    return grid.transpose(0, 2, 1, 3, 4).reshape(rows_n, cols_n, chans)


def contract(left, right, left_dim, right_dim):
    return lax.dot_general(
        left, right, (((left_dim,), (right_dim,)), ((), ())), preferred_element_type=jnp.float32
    )


def window_block(shifted, grad_shifted, gain, w_qkv, w_out, bias_table):
    f32 = jnp.float32
    bf16 = jnp.bfloat16
    rows_n, cols_n, features = shifted.shape
    head_count = bias_table.shape[0]
    window = (bias_table.shape[1] + 1) // 2
    all_heads = w_out.shape[0]
    head_size = all_heads // head_count
    score_scale = head_size ** (-0.5)
    flat_rows = shifted.reshape(rows_n * cols_n, features).astype(f32)
    inverse = lax.rsqrt(jnp.mean(flat_rows * flat_rows, axis=1, keepdims=True) + EPS)
    unit_rows = flat_rows * inverse
    normed = (unit_rows * gain).astype(bf16)
    projected = jnp.dot(normed, w_qkv, preferred_element_type=f32).astype(bf16)
    win_proj = to_windows(projected.reshape(rows_n, cols_n, 3 * all_heads), window)
    count_win = win_proj.shape[0]
    win_proj = win_proj.reshape(count_win, window * window, 3, head_count, head_size)
    queries = win_proj[:, :, 0]
    keys_win = win_proj[:, :, 1]
    values_win = win_proj[:, :, 2]
    row_offset, col_offset = offset_tables(window)
    bias = bias_table[:, row_offset, col_offset]
    scores = (
        jnp.einsum("nqhe,nkhe->nhqk", queries, keys_win, preferred_element_type=f32) * score_scale
        + bias[None]
    )
    peak = jnp.max(scores, axis=-1, keepdims=True)
    expo = jnp.exp(scores - peak)
    softmax_f = expo / jnp.sum(expo, axis=-1, keepdims=True)
    softmax_b = softmax_f.astype(bf16)
    heads_win = jnp.einsum(
        "nhqk,nkhe->nqhe", softmax_b, values_win, preferred_element_type=f32
    ).astype(bf16)
    heads_out = from_windows(
        heads_win.reshape(count_win, window * window, all_heads), rows_n, cols_n, window
    )
    heads_out = heads_out.reshape(rows_n * cols_n, all_heads)
    attention = jnp.dot(heads_out, w_out, preferred_element_type=f32).astype(bf16)
    upstream = grad_shifted.reshape(rows_n * cols_n, features)
    part_out_t = contract(upstream, heads_out, 0, 0)
    grad_heads = contract(upstream, w_out, 1, 1).astype(bf16)
    grad_win = to_windows(grad_heads.reshape(rows_n, cols_n, all_heads), window)
    grad_win = grad_win.reshape(count_win, window * window, head_count, head_size)
    grad_probs = jnp.einsum("nqhe,nkhe->nhqk", grad_win, values_win, preferred_element_type=f32)
    grad_values = jnp.einsum(
        "nhqk,nqhe->nkhe", softmax_b, grad_win, preferred_element_type=f32
    ).astype(bf16)
    inner = jnp.sum(grad_probs * softmax_f, axis=-1, keepdims=True)
    grad_scores = (softmax_f * (grad_probs - inner) * score_scale).astype(bf16)
    grad_queries = jnp.einsum(
        "nhqk,nkhe->nqhe", grad_scores, keys_win, preferred_element_type=f32
    ).astype(bf16)
    grad_keys = jnp.einsum(
        "nhqk,nqhe->nkhe", grad_scores, queries, preferred_element_type=f32
    ).astype(bf16)
    grad_projected = jnp.stack([grad_queries, grad_keys, grad_values], axis=2)
    grad_projected = grad_projected.reshape(count_win, window * window, 3 * all_heads)
    grad_projected = from_windows(grad_projected, rows_n, cols_n, window).reshape(
        rows_n * cols_n, 3 * all_heads
    )
    part_qkv = contract(normed, grad_projected, 0, 0)
    grad_normed = contract(grad_projected, w_qkv, 1, 1)
    part_gain = jnp.sum(grad_normed * unit_rows, axis=0)
    grad_unit = grad_normed * gain
    grad_tokens = inverse * (
        grad_unit - unit_rows * jnp.mean(grad_unit * unit_rows, axis=1, keepdims=True)
    )
    grad_tokens = grad_tokens.astype(bf16)
    return (
        attention.reshape(rows_n, cols_n, features),
        grad_tokens.reshape(rows_n, cols_n, features),
        part_qkv,
        part_out_t,
        part_gain,
    )


def pull_rows(paired):
    rim_rows = passed_along(paired[:, :SHIFT], "rows", -1)
    return jnp.concatenate([paired[:, SHIFT:], rim_rows], axis=1)


def pull_cols(paired):
    rim_cols = passed_along(paired[:, :, :SHIFT], "cols", -1)
    return jnp.concatenate([paired[:, :, SHIFT:], rim_cols], axis=2)


def push_rows(paired):
    rim_rows = passed_along(paired[:, -SHIFT:], "rows", 1)
    return jnp.concatenate([rim_rows, paired[:, :-SHIFT]], axis=1)


def push_cols(paired):
    rim_cols = passed_along(paired[:, :, -SHIFT:], "cols", 1)
    return jnp.concatenate([rim_cols, paired[:, :, :-SHIFT]], axis=2)


def rs_kernel(nz, nx, m_ref, out_ref, recv0, acc_x, acc_y, acc_z,
              rx1, ax1, rx2, ax2, rx3, ry1, ay1, ry2, ay2, ry3, rz1, az1, rz2, az2, rz3,
              swap_out, swap_in, sends, recvs):
    f32, bf16 = jnp.float32, jnp.bfloat16
    row, col, x = lax.axis_index("rows"), lax.axis_index("cols"), lax.axis_index("rep")
    yh, z = row // nz, row % nz
    yl, core = col // 2, col % 2
    y = yh * 2 + yl
    slot = iter(range(1000))
    pair = (row, yl * 2 + 1 - core, x)

    def on_x(step):
        other = (x + step) % nx
        return other, (row, col, other)

    def on_y(step):
        other = (y + step) % 4
        return (other // 2, other % 2), ((other // 2) * nz + z, (other % 2) * 2 + core, x)

    def on_z(step):
        other = (z + step) % nz
        return other, (yh * nz + other, col, x)

    barrier = pltpu.get_barrier_semaphore()
    peers = [pair]
    peers += [on_x(step)[1] for step in range(1, nx)]
    peers += [on_y(step)[1] for step in range(1, 4)]
    peers += [on_z(step)[1] for step in range(1, nz)]
    for peer in peers:
        pl.semaphore_signal(barrier, inc=1, device_id=peer, device_id_type=MESH)
    pl.semaphore_wait(barrier, len(peers))

    started = []

    def send(source, target, device):
        index = next(slot)
        copy = pltpu.make_async_remote_copy(
            src_ref=source, dst_ref=target, send_sem=sends.at[index], recv_sem=recvs.at[index],
            device_id=device, device_id_type=MESH)
        copy.start()
        started.append(copy)
        return copy

    cols_z, cols_x, cols_y = pl.ds(1536, 512), pl.ds(0, 1024), pl.ds(1024, 512)
    first = {}
    for name, cols in (("z", cols_z), ("x", cols_x), ("y", cols_y)):
        first[name] = send(m_ref.at[:, :, :, 1 - core, :, cols], recv0.at[:, :, :, :, cols], pair)

    def add_pair(name):
        first[name].wait_recv()

        def body(block, carry):
            a, b, c = block // (2 * nz), (block // 2) % nz, block % 2
            if name == "z":
                acc_z[a, b, c] = m_ref[a, b, c, core, :, 1536:2048] + recv0[a, b, c, :, 1536:2048]
            elif name == "y":
                acc_y[a, b, c] = m_ref[a, b, c, core, :, 1024:1536] + recv0[a, b, c, :, 1024:1536]
            else:
                wide = 1024 // nx
                for part in range(nx):
                    lo = part * wide
                    acc_x[part, a, b, c] = m_ref[a, b, c, core, :, lo:lo + wide] + recv0[a, b, c, :, lo:lo + wide]
            return carry

        lax.fori_loop(0, 4 * nz, body, 0)

    def landed(copies):
        for copy in copies:
            copy.wait_recv()

    def total(own, slots, count):
        value = own.astype(f32)
        for k in range(count):
            value = value + slots[k].astype(f32)
        return value

    add_pair("z")
    z1 = [send(acc_z.at[:, on_z(s)[0]], rz1.at[s - 1], on_z(s)[1]) for s in range(1, nz)]
    add_pair("x")
    x1 = [send(acc_x.at[on_x(s)[0]], rx1.at[s - 1], on_x(s)[1]) for s in range(1, nx)]
    add_pair("y")
    y1 = [send(acc_y.at[on_y(s)[0][0], :, on_y(s)[0][1]], ry1.at[s - 1], on_y(s)[1]) for s in range(1, 4)]

    landed(y1)

    def body_y1(b, carry):
        ay1[b] = total(acc_y[yh, b, yl], [ry1[k, b] for k in range(3)], 3).astype(bf16)
        return carry

    lax.fori_loop(0, nz, body_y1, 0)
    y2 = [send(ay1.at[on_z(s)[0]], ry2.at[s - 1], on_z(s)[1]) for s in range(1, nz)]

    landed(x1)

    def body_x1(block, carry):
        a, b, c = block // (2 * nz), (block // 2) % nz, block % 2
        ax1[a, b, c] = total(acc_x[x, a, b, c], [rx1[k, a, b, c] for k in range(nx - 1)], nx - 1).astype(bf16)
        return carry

    lax.fori_loop(0, 4 * nz, body_x1, 0)
    x2 = [send(ax1.at[on_y(s)[0][0], :, on_y(s)[0][1]], rx2.at[s - 1], on_y(s)[1]) for s in range(1, 4)]

    landed(z1)
    for a in range(2):
        for c in range(2):
            value = total(acc_z[a, z, c], [rz1[k, a, c] for k in range(nz - 1)], nz - 1).astype(bf16)
            wide = 512 // nx
            for part in range(nx):
                az1[part, a, c] = value[:, part * wide:(part + 1) * wide]
    z2 = [send(az1.at[on_x(s)[0]], rz2.at[s - 1], on_x(s)[1]) for s in range(1, nx)]

    landed(y2)
    value = total(ay1[z], [ry2[k] for k in range(nz - 1)], nz - 1).astype(bf16)
    wide = 512 // nx
    for part in range(nx):
        ay2[part] = value[:, part * wide:(part + 1) * wide]
    y3 = [send(ay2.at[on_x(s)[0]], ry3.at[s - 1], on_x(s)[1]) for s in range(1, nx)]
    landed(x2)

    def body_x2(b, carry):
        ax2[b] = total(ax1[yh, b, yl], [rx2[k, b] for k in range(3)], 3).astype(bf16)
        return carry

    lax.fori_loop(0, nz, body_x2, 0)
    x3 = [send(ax2.at[on_z(s)[0]], rx3.at[s - 1], on_z(s)[1]) for s in range(1, nz)]
    landed(z2)
    for a in range(2):
        for c in range(2):
            az2[a, c] = total(az1[x, a, c], [rz2[k, a, c] for k in range(nx - 1)], nx - 1).astype(bf16)
    z3 = [send(az2.at[on_y(s)[0][0], on_y(s)[0][1]], rz3.at[s - 1], on_y(s)[1]) for s in range(1, 4)]

    landed(y3)
    sum_y = total(ay2[x], [ry3[k] for k in range(nx - 1)], nx - 1)
    landed(z3)
    sum_z = total(az2[yh, yl], [rz3[k] for k in range(3)], 3)
    landed(x3)
    sum_x = total(ax2[z], [rx3[k] for k in range(nz - 1)], nz - 1)
    rest = jnp.concatenate([sum_y, sum_z], axis=1)
    for other in range(nx):
        swap_out[other, 0:4] = sum_x[other * 4:other * 4 + 4]
        swap_out[other, 4:8] = rest[other * 4:other * 4 + 4]
    last = [send(swap_out.at[on_x(s)[0]], swap_in.at[s - 1], on_x(s)[1]) for s in range(1, nx)]
    swap_in[nx - 1] = swap_out[x]
    landed(last)
    for source in range(nx):
        k = (x - source + nx - 1) % nx
        got = swap_in[k]
        wx, wr = 1024 // nx, 512 // nx
        out_ref[:, source * wx:(source + 1) * wx] = got[0:4]
        out_ref[:, 1024 + source * wr:1024 + (source + 1) * wr] = got[4:8, 0:wr]
        out_ref[:, 1536 + source * wr:1536 + (source + 1) * wr] = got[4:8, wr:2 * wr]
    for copy in started:
        copy.wait_send()


def reduce_scatter(partial, nz, nx):
    bf16, f32 = jnp.bfloat16, jnp.float32
    wx, wr = 1024 // nx, 512 // nx
    shapes = [
        ((2, nz, 2, 16, 2048), bf16),
        ((nx, 2, nz, 2, 16, wx), bf16), ((2, nz, 2, 16, 512), bf16), ((2, nz, 2, 16, 512), bf16),
        ((nx - 1, 2, nz, 2, 16, wx), bf16), ((2, nz, 2, 16, wx), bf16),
        ((3, nz, 16, wx), bf16), ((nz, 16, wx), bf16), ((nz - 1, 16, wx), bf16),
        ((3, nz, 16, 512), bf16), ((nz, 16, 512), bf16),
        ((nz - 1, 16, 512), bf16), ((nx, 16, wr), bf16), ((nx - 1, 16, wr), bf16),
        ((nz - 1, 2, 2, 16, 512), bf16), ((nx, 2, 2, 16, wr), bf16),
        ((nx - 1, 2, 2, 16, wr), bf16), ((2, 2, 16, wr), bf16), ((3, 16, wr), bf16),
        ((nx, 8, wx), f32), ((nx, 8, wx), f32),
    ]
    copies = 3 + (nz - 1 + nx - 1 + 3) * 3 + nx - 1
    return pl.pallas_call(
        functools.partial(rs_kernel, nz, nx),
        out_shape=jax.ShapeDtypeStruct((4, 2048), f32),
        in_specs=[pl.BlockSpec(memory_space=pltpu.VMEM)],
        out_specs=pl.BlockSpec(memory_space=pltpu.VMEM),
        scratch_shapes=[pltpu.VMEM(shape, kind) for shape, kind in shapes]
        + [pltpu.SemaphoreType.DMA((copies,)), pltpu.SemaphoreType.DMA((copies,))],
        compiler_params=pltpu.CompilerParams(
            collective_id=0, has_side_effects=True, vmem_limit_bytes=40 * 1024 * 1024),
        name="reduce_scatter",
    )(partial.reshape(2, nz, 2, 2, 16, 2048))


def local(image, cotangent, gain, w_qkv, w_out, bias_table):
    f32 = jnp.float32
    paired = jnp.stack([image[0], cotangent[0]])
    shifted = pull_cols(pull_rows(paired))
    attention, grad_tokens, part_qkv, part_out_t, part_gain = window_block(
        shifted[0], shifted[1], gain, w_qkv, w_out, bias_table
    )
    branch = jnp.stack([attention, grad_tokens])
    returned = push_cols(push_rows(branch))
    result = (image[0].astype(f32) + returned[0].astype(f32)).astype(jnp.bfloat16)
    grad_result = (cotangent[0].astype(f32) + returned[1].astype(f32)).astype(jnp.bfloat16)
    partial = jnp.concatenate([part_qkv.astype(jnp.bfloat16), part_out_t.astype(jnp.bfloat16)], axis=1)
    summed = reduce_scatter(partial, lax.axis_size("rows") // 2, lax.axis_size("rep"))
    total_count = (
        lax.axis_size("rows")
        * lax.axis_size("cols")
        * lax.axis_size("rep")
        * image.shape[1]
        * image.shape[2]
    )
    factor = 1.0 / float(np.sqrt(total_count))
    grad_qkv = summed[:, :1536] * factor
    first = 4 * ((lax.axis_index("rows") * 4 + lax.axis_index("cols")) * 4 + lax.axis_index("rep"))
    own_w = lax.dynamic_slice_in_dim(w_qkv, first, 4, 0).astype(f32)
    own_gain = lax.dynamic_slice_in_dim(gain, first, 4, 0)
    grad_gain = jnp.sum(own_w * grad_qkv, axis=1) / own_gain
    return (
        result[None],
        grad_result[None],
        grad_qkv,
        (summed[:, 1536:] * factor).T,
        grad_gain,
    )


def solution(mesh):
    in_specs = (P("rep", "rows", "cols", None), P("rep", "rows", "cols", None), P(), P(), P(), P())
    out_specs = (
        P("rep", "rows", "cols", None),
        P("rep", "rows", "cols", None),
        P(("rows", "cols", "rep"), None),
        P(None, ("rows", "cols", "rep")),
        P(("rows", "cols", "rep")),
    )
    return jax.shard_map(local, mesh=mesh, in_specs=in_specs, out_specs=out_specs, check_vma=False)
```

```python
import functools

import jax
import jax.numpy as jnp
import numpy as np
from jax import lax
from jax.experimental import pallas as pl
from jax.experimental.pallas import tpu as pltpu
from jax.sharding import PartitionSpec as P

MESH = pl.DeviceIdType.MESH
SHIFT = 4
EPS = 1e-06


def passed_along(value, axis, steps):
    count = lax.axis_size(axis)
    pairs = [(source, (source + steps) % count) for source in range(count)]
    return lax.ppermute(value, axis, pairs)


def to_blocks(tile):
    rows, cols, features = tile.shape
    blocks = tile.reshape(rows // 4, 4, cols // 4, 4, features)
    return blocks.transpose(0, 2, 1, 3, 4).reshape(rows // 4, cols // 4, 16, features)


def from_blocks(blocks):
    brows, bcols, _, features = blocks.shape
    tile = blocks.reshape(brows, bcols, 4, 4, features).transpose(0, 2, 1, 3, 4)
    return tile.reshape(brows * 4, bcols * 4, features)


def pull(paired):
    rim = passed_along(paired[:, :1], "rows", -1)
    paired = jnp.concatenate([paired[:, 1:], rim], axis=1)
    rim = passed_along(paired[:, :, :1], "cols", -1)
    return jnp.concatenate([paired[:, :, 1:], rim], axis=2)


def push(paired):
    rim = passed_along(paired[:, -1:], "rows", 1)
    paired = jnp.concatenate([rim, paired[:, :-1]], axis=1)
    rim = passed_along(paired[:, :, -1:], "cols", 1)
    return jnp.concatenate([rim, paired[:, :, :-1]], axis=2)


def windows(blocks):
    brows, bcols, size, features = blocks.shape
    value = blocks.reshape(brows // 2, 2, bcols // 2, 2, size, features)
    return value.transpose(0, 2, 1, 3, 4, 5).reshape(brows * bcols * size, features)


def unwindows(tokens, brows, bcols):
    value = tokens.reshape(brows // 2, bcols // 2, 2, 2, 16, tokens.shape[-1])
    return value.transpose(0, 2, 1, 3, 4, 5).reshape(brows, bcols, 16, tokens.shape[-1])


def token_place(index):
    return (index // 32) * 4 + (index % 16) // 4, ((index // 16) % 2) * 4 + index % 4


def nt(left, right):
    return lax.dot_general(left, right, (((1,), (1,)), ((), ())), preferred_element_type=jnp.float32)


def tn(left, right):
    return lax.dot_general(left, right, (((0,), (0,)), ((), ())), preferred_element_type=jnp.float32)


def block_kernel(x_ref, g_ref, gain_ref, wqkv_ref, wout_ref, table_ref,
                 att_ref, gtok_ref, part_ref,
                 norm_t, g_t, inv_ref, proj, gheads, heads, gproj, bias_ref):
    f32, bf16 = jnp.float32, jnp.bfloat16
    i32 = jnp.int32
    tokens, features = x_ref.shape
    head_dim, group = 64, 256
    all_heads = wout_ref.shape[0]
    scale = head_dim ** -0.5
    rows = 128

    krow, kcol = token_place(lax.broadcasted_iota(i32, (64, 128), 0))
    qrow, qcol = token_place(lax.broadcasted_iota(i32, (64, 128), 1) % 64)
    offset = (qrow - krow + 7) * 16 + qcol - kcol + 7
    low, low_half = offset % 128, offset < 128
    first_head = lax.broadcasted_iota(i32, (64, 128), 1) < 64

    def bias_of(head):
        a = jnp.broadcast_to(table_ref[head:head + 1, 0:128], (64, 128))
        b = jnp.broadcast_to(table_ref[head:head + 1, 128:256], (64, 128))
        at = functools.partial(jnp.take_along_axis, indices=low, axis=1, mode="promise_in_bounds")
        return jnp.where(low_half, at(a), at(b))

    for duo in range(all_heads // 128):
        bias_ref[duo // 2, :, (duo % 2) * 128:(duo % 2) * 128 + 128] = jnp.where(
            first_head, bias_of(2 * duo), bias_of(2 * duo + 1))

    def project(step, carry):
        part = pl.ds(pl.multiple_of(step * rows, rows), rows)
        value = x_ref[part, :].astype(f32)
        inverse = lax.rsqrt(jnp.mean(value * value, axis=1, keepdims=True) + EPS)
        inv_ref[part, :] = inverse
        normed = (value * inverse * gain_ref[...]).astype(bf16)
        upstream = g_ref[part, :]
        norm_t[step] = normed.T
        g_t[step] = upstream.T
        proj[part, :] = jnp.dot(normed, wqkv_ref[...], preferred_element_type=f32).astype(bf16)
        gheads[part, :] = nt(upstream, wout_ref[...]).astype(bf16)
        return carry

    lax.fori_loop(0, tokens // rows, project, 0)

    head_row = lax.broadcasted_iota(i32, (group, group), 0) // head_dim
    head_lane = lax.broadcasted_iota(i32, (group, group), 1) // head_dim
    diagonal = head_row == head_lane
    lane64 = lax.broadcasted_iota(i32, (64, group), 1) // head_dim

    def spread(value):
        return jnp.where(diagonal, jnp.concatenate([value] * 4, axis=0), jnp.zeros((), value.dtype))

    def gather_heads(full):
        out = full[0:64]
        for h in range(1, 4):
            out = jnp.where(lane64 == h, full[h * 64:h * 64 + 64], out)
        return out

    def attend(win, carry):
        part = pl.ds(pl.multiple_of(win * 64, 64), 64)
        for grp in range(all_heads // group):
            lo = grp * group
            q = proj[part, lo:lo + group]
            k = proj[part, all_heads + lo:all_heads + lo + group]
            v = proj[part, 2 * all_heads + lo:2 * all_heads + lo + group]
            go = gheads[part, lo:lo + group]
            q_wide, go_wide = spread(q), spread(go)
            scores = nt(k, q_wide) * scale + bias_ref[grp]
            expo = jnp.exp(scores - jnp.max(scores, axis=0, keepdims=True))
            soft = expo * (1.0 / jnp.sum(expo, axis=0, keepdims=True))
            soft_b = soft.astype(bf16)
            gp = nt(v, go_wide)
            inner = jnp.sum(gp * soft, axis=0, keepdims=True)
            gs = (soft * (gp - inner) * scale).astype(bf16)
            heads[part, lo:lo + group] = gather_heads(tn(soft_b, v)).astype(bf16)
            gproj[part, lo:lo + group] = gather_heads(tn(gs, k)).astype(bf16)
            gproj[part, all_heads + lo:all_heads + lo + group] = jnp.dot(
                gs, q_wide, preferred_element_type=f32).astype(bf16)
            gproj[part, 2 * all_heads + lo:2 * all_heads + lo + group] = jnp.dot(
                soft_b, go_wide, preferred_element_type=f32).astype(bf16)
        return carry

    lax.fori_loop(0, tokens // 64, attend, 0)

    def weights(step, carry):
        part = pl.ds(pl.multiple_of(step * rows, rows), rows)
        left = jnp.concatenate([norm_t[t, part, :] for t in range(tokens // rows)], axis=1)
        part_ref[part, 0:3 * all_heads] = jnp.dot(left, gproj[...], preferred_element_type=f32).astype(bf16)
        left = jnp.concatenate([g_t[t, part, :] for t in range(tokens // rows)], axis=1)
        part_ref[part, 3 * all_heads:] = jnp.dot(left, heads[...], preferred_element_type=f32).astype(bf16)
        return carry

    lax.fori_loop(0, features // rows, weights, 0)

    def finish(step, carry):
        part = pl.ds(pl.multiple_of(step * rows, rows), rows)
        att_ref[part, :] = jnp.dot(heads[part, :], wout_ref[...], preferred_element_type=f32).astype(bf16)
        grad_normed = nt(gproj[part, :], wqkv_ref[...])
        inverse = inv_ref[part, :]
        unit = x_ref[part, :].astype(f32) * inverse
        grad_unit = grad_normed * gain_ref[...]
        mean = jnp.mean(grad_unit * unit, axis=1, keepdims=True)
        gtok_ref[part, :] = (inverse * (grad_unit - unit * mean)).astype(bf16)
        return carry

    lax.fori_loop(0, tokens // rows, finish, 0)


def window_block(x, g, gain, w_qkv, w_out, bias_table):
    f32, bf16 = jnp.float32, jnp.bfloat16
    tokens, features = x.shape
    all_heads = w_out.shape[0]
    table = jnp.pad(bias_table, ((0, 0), (0, 1), (0, 1))).reshape(bias_table.shape[0], 256)
    vmem = pl.BlockSpec(memory_space=pltpu.VMEM)
    return pl.pallas_call(
        block_kernel,
        out_shape=(
            jax.ShapeDtypeStruct((tokens, features), bf16),
            jax.ShapeDtypeStruct((tokens, features), bf16),
            jax.ShapeDtypeStruct((features, 4 * all_heads), bf16),
        ),
        in_specs=[vmem] * 6,
        out_specs=(vmem,) * 3,
        scratch_shapes=[
            pltpu.VMEM((tokens // 128, features, 128), bf16),
            pltpu.VMEM((tokens // 128, features, 128), bf16),
            pltpu.VMEM((tokens, 1), f32),
            pltpu.VMEM((tokens, 3 * all_heads), bf16),
            pltpu.VMEM((tokens, all_heads), bf16),
            pltpu.VMEM((tokens, all_heads), bf16),
            pltpu.VMEM((tokens, 3 * all_heads), bf16),
            pltpu.VMEM((2, 64, 256), f32),
        ],
        compiler_params=pltpu.CompilerParams(vmem_limit_bytes=48 * 1024 * 1024),
        name="window_block",
    )(x, g, gain.reshape(1, features), w_qkv, w_out, table)


def rs_kernel(nz, nx, m_ref, out_ref, recv0, acc_x, acc_y, acc_z,
              rx1, ax1, rx2, ax2, rx3, ry1, ay1, ry2, ay2, ry3, rz1, az1, rz2, az2, rz3,
              swap_out, swap_in, sends, recvs):
    f32, bf16 = jnp.float32, jnp.bfloat16
    row, col, x = lax.axis_index("rows"), lax.axis_index("cols"), lax.axis_index("rep")
    yh, z = row // nz, row % nz
    yl, core = col // 2, col % 2
    y = yh * 2 + yl
    slot = iter(range(1000))
    pair = (row, yl * 2 + 1 - core, x)

    def on_x(step):
        other = (x + step) % nx
        return other, (row, col, other)

    def on_y(step):
        other = (y + step) % 4
        return (other // 2, other % 2), ((other // 2) * nz + z, (other % 2) * 2 + core, x)

    def on_z(step):
        other = (z + step) % nz
        return other, (yh * nz + other, col, x)

    barrier = pltpu.get_barrier_semaphore()
    peers = [pair]
    peers += [on_x(step)[1] for step in range(1, nx)]
    peers += [on_y(step)[1] for step in range(1, 4)]
    peers += [on_z(step)[1] for step in range(1, nz)]
    for peer in peers:
        pl.semaphore_signal(barrier, inc=1, device_id=peer, device_id_type=MESH)
    pl.semaphore_wait(barrier, len(peers))

    started = []

    def send(source, target, device):
        index = next(slot)
        copy = pltpu.make_async_remote_copy(
            src_ref=source, dst_ref=target, send_sem=sends.at[index], recv_sem=recvs.at[index],
            device_id=device, device_id_type=MESH)
        copy.start()
        started.append(copy)
        return copy

    cols_z, cols_x, cols_y = pl.ds(1536, 512), pl.ds(0, 1024), pl.ds(1024, 512)
    first = {}
    for name, cols in (("z", cols_z), ("x", cols_x), ("y", cols_y)):
        first[name] = send(m_ref.at[:, :, :, 1 - core, :, cols], recv0.at[:, :, :, :, cols], pair)

    def add_pair(name):
        first[name].wait_recv()

        def body(block, carry):
            a, b, c = block // (2 * nz), (block // 2) % nz, block % 2
            if name == "z":
                acc_z[a, b, c] = m_ref[a, b, c, core, :, 1536:2048] + recv0[a, b, c, :, 1536:2048]
            elif name == "y":
                acc_y[a, b, c] = m_ref[a, b, c, core, :, 1024:1536] + recv0[a, b, c, :, 1024:1536]
            else:
                wide = 1024 // nx
                for part in range(nx):
                    lo = part * wide
                    acc_x[part, a, b, c] = m_ref[a, b, c, core, :, lo:lo + wide] + recv0[a, b, c, :, lo:lo + wide]
            return carry

        lax.fori_loop(0, 4 * nz, body, 0)

    def landed(copies):
        for copy in copies:
            copy.wait_recv()

    def total(own, slots, count):
        value = own.astype(f32)
        for k in range(count):
            value = value + slots[k].astype(f32)
        return value

    add_pair("z")
    z1 = [send(acc_z.at[:, on_z(s)[0]], rz1.at[s - 1], on_z(s)[1]) for s in range(1, nz)]
    add_pair("x")
    x1 = [send(acc_x.at[on_x(s)[0]], rx1.at[s - 1], on_x(s)[1]) for s in range(1, nx)]
    add_pair("y")
    y1 = [send(acc_y.at[on_y(s)[0][0], :, on_y(s)[0][1]], ry1.at[s - 1], on_y(s)[1]) for s in range(1, 4)]

    landed(y1)

    def body_y1(b, carry):
        ay1[b] = total(acc_y[yh, b, yl], [ry1[k, b] for k in range(3)], 3).astype(bf16)
        return carry

    lax.fori_loop(0, nz, body_y1, 0)
    y2 = [send(ay1.at[on_z(s)[0]], ry2.at[s - 1], on_z(s)[1]) for s in range(1, nz)]

    landed(x1)

    def body_x1(block, carry):
        a, b, c = block // (2 * nz), (block // 2) % nz, block % 2
        ax1[a, b, c] = total(acc_x[x, a, b, c], [rx1[k, a, b, c] for k in range(nx - 1)], nx - 1).astype(bf16)
        return carry

    lax.fori_loop(0, 4 * nz, body_x1, 0)
    x2 = [send(ax1.at[on_y(s)[0][0], :, on_y(s)[0][1]], rx2.at[s - 1], on_y(s)[1]) for s in range(1, 4)]

    landed(z1)
    for a in range(2):
        for c in range(2):
            value = total(acc_z[a, z, c], [rz1[k, a, c] for k in range(nz - 1)], nz - 1).astype(bf16)
            wide = 512 // nx
            for part in range(nx):
                az1[part, a, c] = value[:, part * wide:(part + 1) * wide]
    z2 = [send(az1.at[on_x(s)[0]], rz2.at[s - 1], on_x(s)[1]) for s in range(1, nx)]

    landed(y2)
    value = total(ay1[z], [ry2[k] for k in range(nz - 1)], nz - 1).astype(bf16)
    wide = 512 // nx
    for part in range(nx):
        ay2[part] = value[:, part * wide:(part + 1) * wide]
    y3 = [send(ay2.at[on_x(s)[0]], ry3.at[s - 1], on_x(s)[1]) for s in range(1, nx)]
    landed(x2)

    def body_x2(b, carry):
        ax2[b] = total(ax1[yh, b, yl], [rx2[k, b] for k in range(3)], 3).astype(bf16)
        return carry

    lax.fori_loop(0, nz, body_x2, 0)
    x3 = [send(ax2.at[on_z(s)[0]], rx3.at[s - 1], on_z(s)[1]) for s in range(1, nz)]
    landed(z2)
    for a in range(2):
        for c in range(2):
            az2[a, c] = total(az1[x, a, c], [rz2[k, a, c] for k in range(nx - 1)], nx - 1).astype(bf16)
    z3 = [send(az2.at[on_y(s)[0][0], on_y(s)[0][1]], rz3.at[s - 1], on_y(s)[1]) for s in range(1, 4)]

    landed(y3)
    sum_y = total(ay2[x], [ry3[k] for k in range(nx - 1)], nx - 1)
    landed(z3)
    sum_z = total(az2[yh, yl], [rz3[k] for k in range(3)], 3)
    landed(x3)
    sum_x = total(ax2[z], [rx3[k] for k in range(nz - 1)], nz - 1)
    rest = jnp.concatenate([sum_y, sum_z], axis=1)
    for other in range(nx):
        swap_out[other, 0:4] = sum_x[other * 4:other * 4 + 4]
        swap_out[other, 4:8] = rest[other * 4:other * 4 + 4]
    last = [send(swap_out.at[on_x(s)[0]], swap_in.at[s - 1], on_x(s)[1]) for s in range(1, nx)]
    swap_in[nx - 1] = swap_out[x]
    landed(last)
    for source in range(nx):
        k = (x - source + nx - 1) % nx
        got = swap_in[k]
        wx, wr = 1024 // nx, 512 // nx
        out_ref[:, source * wx:(source + 1) * wx] = got[0:4]
        out_ref[:, 1024 + source * wr:1024 + (source + 1) * wr] = got[4:8, 0:wr]
        out_ref[:, 1536 + source * wr:1536 + (source + 1) * wr] = got[4:8, wr:2 * wr]
    for copy in started:
        copy.wait_send()


def reduce_scatter(partial, nz, nx):
    bf16, f32 = jnp.bfloat16, jnp.float32
    wx, wr = 1024 // nx, 512 // nx
    shapes = [
        ((2, nz, 2, 16, 2048), bf16),
        ((nx, 2, nz, 2, 16, wx), bf16), ((2, nz, 2, 16, 512), bf16), ((2, nz, 2, 16, 512), bf16),
        ((nx - 1, 2, nz, 2, 16, wx), bf16), ((2, nz, 2, 16, wx), bf16),
        ((3, nz, 16, wx), bf16), ((nz, 16, wx), bf16), ((nz - 1, 16, wx), bf16),
        ((3, nz, 16, 512), bf16), ((nz, 16, 512), bf16),
        ((nz - 1, 16, 512), bf16), ((nx, 16, wr), bf16), ((nx - 1, 16, wr), bf16),
        ((nz - 1, 2, 2, 16, 512), bf16), ((nx, 2, 2, 16, wr), bf16),
        ((nx - 1, 2, 2, 16, wr), bf16), ((2, 2, 16, wr), bf16), ((3, 16, wr), bf16),
        ((nx, 8, wx), f32), ((nx, 8, wx), f32),
    ]
    copies = 3 + (nz - 1 + nx - 1 + 3) * 3 + nx - 1
    return pl.pallas_call(
        functools.partial(rs_kernel, nz, nx),
        out_shape=jax.ShapeDtypeStruct((4, 2048), f32),
        in_specs=[pl.BlockSpec(memory_space=pltpu.VMEM)],
        out_specs=pl.BlockSpec(memory_space=pltpu.VMEM),
        scratch_shapes=[pltpu.VMEM(shape, kind) for shape, kind in shapes]
        + [pltpu.SemaphoreType.DMA((copies,)), pltpu.SemaphoreType.DMA((copies,))],
        compiler_params=pltpu.CompilerParams(
            collective_id=0, has_side_effects=True, vmem_limit_bytes=40 * 1024 * 1024),
        name="reduce_scatter",
    )(partial.reshape(2, nz, 2, 2, 16, 2048))


def local(image, cotangent, gain, w_qkv, w_out, bias_table):
    f32 = jnp.float32
    blocks = jnp.stack([to_blocks(image[0]), to_blocks(cotangent[0])])
    shifted = pull(blocks)
    attention, grad_tokens, partial = window_block(
        windows(shifted[0]), windows(shifted[1]), gain, w_qkv, w_out, bias_table
    )
    brows, bcols = blocks.shape[1:3]
    returned = push(jnp.stack([unwindows(attention, brows, bcols), unwindows(grad_tokens, brows, bcols)]))
    result = (image[0].astype(f32) + from_blocks(returned[0]).astype(f32)).astype(jnp.bfloat16)
    grad_result = (cotangent[0].astype(f32) + from_blocks(returned[1]).astype(f32)).astype(jnp.bfloat16)
    summed = reduce_scatter(partial, lax.axis_size("rows") // 2, lax.axis_size("rep"))
    total_count = (
        lax.axis_size("rows")
        * lax.axis_size("cols")
        * lax.axis_size("rep")
        * image.shape[1]
        * image.shape[2]
    )
    factor = 1.0 / float(np.sqrt(total_count))
    grad_qkv = summed[:, :1536] * factor
    first = 4 * ((lax.axis_index("rows") * 4 + lax.axis_index("cols")) * 4 + lax.axis_index("rep"))
    own_w = lax.dynamic_slice_in_dim(w_qkv, first, 4, 0).astype(f32)
    own_gain = lax.dynamic_slice_in_dim(gain, first, 4, 0)
    grad_gain = jnp.sum(own_w * grad_qkv, axis=1) / own_gain
    return (
        result[None],
        grad_result[None],
        grad_qkv,
        (summed[:, 1536:] * factor).T,
        grad_gain,
    )


def solution(mesh):
    in_specs = (P("rep", "rows", "cols", None), P("rep", "rows", "cols", None), P(), P(), P(), P())
    out_specs = (
        P("rep", "rows", "cols", None),
        P("rep", "rows", "cols", None),
        P(("rows", "cols", "rep"), None),
        P(None, ("rows", "cols", "rep")),
        P(("rows", "cols", "rep")),
    )
    return jax.shard_map(local, mesh=mesh, in_specs=in_specs, out_specs=out_specs, check_vma=False)
```

```python
import functools

import jax
import jax.numpy as jnp
import numpy as np
from jax import lax
from jax.experimental import pallas as pl
from jax.experimental.pallas import tpu as pltpu
from jax.sharding import PartitionSpec as P

MESH = pl.DeviceIdType.MESH
EPS = 1e-06
GROUP = 256
HEAD = 64
PARTS = (("zxy", 0, 0), ("xyz", 0, 512), ("yzx", 1, 0), ("xyz", 1, 512))


def token_place(index):
    return (index // 32) * 4 + (index % 16) // 4, ((index // 16) % 2) * 4 + index % 4


def nt(left, right):
    return lax.dot_general(left, right, (((1,), (1,)), ((), ())), preferred_element_type=jnp.float32)


def tn(left, right):
    return lax.dot_general(left, right, (((0,), (0,)), ((), ())), preferred_element_type=jnp.float32)


def nn(left, right):
    return jnp.dot(left, right, preferred_element_type=jnp.float32)


def block_place(rb, cb):
    if cb == 0:
        return ("corner", 0, 0) if rb == 3 else ("left", rb, 0)
    if rb in (1, 2):
        return ("window", 3, (rb - 1) * 2) if cb == 7 else ("window", (cb - 1) // 2, (rb - 1) * 2 + (cb - 1) % 2)
    if rb == 3:
        return ("window", 4 + (cb - 1) // 2, (cb - 1) % 2) if cb <= 4 else ("down", cb - 5, 0)
    if cb <= 4:
        return ("up", (cb - 1) // 2, (cb - 1) % 2)
    return ("window", 7, 2) if cb == 7 else ("window", 6, 2 + cb - 5)


def kernel(nz, nx, factor,
           img_ref, cot_ref, gain_ref, wqkv_hbm, wout_hbm, table_ref,
           out_ref, gimg_ref, gqkv_ref, gout_ref, ggain_ref,
           wqkv_ref, wout_ref, tok, ret,
           up, down, left, corner, b_up, b_down, b_left, b_corner,
           norm_t, g_t, inv_ref, proj, gheads, heads, gproj, bias_ref,
           m_ref, recv0, *rest):
    f32, bf16, i32 = jnp.float32, jnp.bfloat16, jnp.int32
    count_parts = len(PARTS)
    acc1, acc2, acc3 = rest[0:4], rest[4:8], rest[8:12]
    rx1, rx2, rx3 = rest[12:16], rest[16:20], rest[20:24]
    swap_out, swap_in, sends, recvs, local_sems = rest[24:]
    scale = HEAD ** -0.5
    all_heads = 2 * GROUP

    row, col, x = lax.axis_index("rows"), lax.axis_index("cols"), lax.axis_index("rep")
    yh, z = row // nz, row % nz
    yl, core = col // 2, col % 2
    y = yh * 2 + yl
    place = {"x": x, "y": y, "z": z}
    size = {"x": nx, "y": 4, "z": nz}
    pair = (row, yl * 2 + 1 - core, x)
    above = ((row + 2 * nz - 1) % (2 * nz), col, x)
    below = ((row + 1) % (2 * nz), col, x)
    lefty = (row, (col + 3) % 4, x)
    right = (row, (col + 1) % 4, x)
    below_left = ((row + 1) % (2 * nz), (col + 3) % 4, x)
    above_right = ((row + 2 * nz - 1) % (2 * nz), (col + 1) % 4, x)

    def on(axis, step):
        other = (place[axis] + step) % size[axis]
        if axis == "x":
            return other, (row, col, other)
        if axis == "y":
            return other, ((other // 2) * nz + z, (other % 2) * 2 + core, x)
        return other, (yh * nz + other, col, x)

    copies = [
        pltpu.make_async_copy(wqkv_hbm, wqkv_ref, local_sems.at[0]),
        pltpu.make_async_copy(wout_hbm, wout_ref, local_sems.at[1]),
    ]
    for copy in copies:
        copy.start()

    barrier = pltpu.get_barrier_semaphore()
    peers = [pair, above, below, lefty, right, below_left, above_right]
    for axis in "xyz":
        peers += [on(axis, step)[1] for step in range(1, size[axis])]
    for peer in peers:
        pl.semaphore_signal(barrier, inc=1, device_id=peer, device_id_type=MESH)

    slot = iter(range(1000))
    started = []

    def send(source, target, device):
        index = next(slot)
        copy = pltpu.make_async_remote_copy(
            src_ref=source, dst_ref=target, send_sem=sends.at[index], recv_sem=recvs.at[index],
            device_id=device, device_id_type=MESH)
        copy.start()
        started.append(copy)
        return copy

    def landed(arrivals):
        for copy in arrivals:
            copy.wait_recv()

    rim = {"up": up, "down": down, "left": left, "corner": corner}
    back = {"up": b_up, "down": b_down, "left": b_left, "corner": b_corner}
    one = lax.broadcasted_iota(i32, (128, 128), 0)
    two = lax.broadcasted_iota(i32, (128, 128), 1)
    to_block = (two == ((one % 16) // 4) * 32 + (one // 16) * 4 + one % 4).astype(bf16)
    from_block = (two == ((one % 32) // 4) * 16 + (one // 32) * 4 + one % 4).astype(bf16)

    def block_at(own, rims, which, spot):
        name, a, b = spot
        if name == "window":
            return own.at[which, a, b]
        return rims[name].at[which, a, b]

    for rb in (0, 3, 1, 2):
        for which, ref in ((0, img_ref), (1, cot_ref)):
            value = nn(to_block, ref[rb * 4:rb * 4 + 4].reshape(128, 1024)).astype(bf16)
            for cb in range(8):
                block_at(tok, rim, which, block_place(rb, cb))[...] = value[cb * 16:cb * 16 + 16]

    pl.semaphore_wait(barrier, len(peers))
    from_right = [
        send(left.at[:, 1, 0], tok.at[:, 3, 1], lefty),
        send(left.at[:, 2, 0], tok.at[:, 3, 3], lefty),
    ]
    from_below = [send(up, tok.at[:, 4:6, 2:4], above)]
    from_above = [
        send(down.at[:, 0, 0], tok.at[:, 6, 0], below),
        send(down.at[:, 1, 0], tok.at[:, 6, 1], below),
        send(down.at[:, 2, 0], tok.at[:, 7, 0], below),
        send(corner.at[:, 0, 0], tok.at[:, 7, 1], below_left),
        send(left.at[:, 0, 0], tok.at[:, 7, 3], lefty),
    ]

    krow, kcol = token_place(lax.broadcasted_iota(i32, (64, 128), 0))
    qrow, qcol = token_place(lax.broadcasted_iota(i32, (64, 128), 1) % 64)
    offset = (qrow - krow + 7) * 16 + qcol - kcol + 7
    low, low_half = offset % 128, offset < 128
    first_head = lax.broadcasted_iota(i32, (64, 128), 1) < 64

    def bias_of(head):
        at = functools.partial(jnp.take_along_axis, indices=low, axis=1, mode="promise_in_bounds")
        one_half = at(jnp.broadcast_to(table_ref[head:head + 1, 0:128], (64, 128)))
        return jnp.where(low_half, one_half, at(jnp.broadcast_to(table_ref[head:head + 1, 128:256], (64, 128))))

    for duo in range(4):
        bias_ref[duo // 2, :, (duo % 2) * 128:(duo % 2) * 128 + 128] = jnp.where(
            first_head, bias_of(2 * duo), bias_of(2 * duo + 1))

    def chunk(step):
        return slice(step * 128, step * 128 + 128)

    def project(step):
        part = chunk(step)
        value = tok[0, 2 * step:2 * step + 2].reshape(128, 1024).astype(f32)
        inverse = lax.rsqrt(jnp.mean(value * value, axis=1, keepdims=True) + EPS)
        inv_ref[part, :] = inverse
        normed = (value * inverse * gain_ref[...]).astype(bf16)
        upstream = tok[1, 2 * step:2 * step + 2].reshape(128, 1024)
        norm_t[step] = normed.T
        g_t[step] = upstream.T
        proj[part, :] = nn(normed, wqkv_ref[...]).astype(bf16)
        gheads[part, :] = nt(upstream, wout_ref[...]).astype(bf16)

    head_row = lax.broadcasted_iota(i32, (GROUP, GROUP), 0) // HEAD
    head_lane = lax.broadcasted_iota(i32, (GROUP, GROUP), 1) // HEAD
    diagonal = head_row == head_lane
    lane64 = lax.broadcasted_iota(i32, (64, GROUP), 1) // HEAD

    def spread(value):
        return jnp.where(diagonal, jnp.concatenate([value] * 4, axis=0), jnp.zeros((), value.dtype))

    def gather_heads(full):
        out = full[0:64]
        for h in range(1, 4):
            out = jnp.where(lane64 == h, full[h * 64:h * 64 + 64], out)
        return out

    def attend(win, grp):
        part = pl.ds(pl.multiple_of(win * 64, 64), 64)
        lo = grp * GROUP
        cq = slice(lo, lo + GROUP)
        ck = slice(all_heads + lo, all_heads + lo + GROUP)
        cv = slice(2 * all_heads + lo, 2 * all_heads + lo + GROUP)
        q, k, v, go = proj[part, cq], proj[part, ck], proj[part, cv], gheads[part, cq]
        q_wide, go_wide = spread(q), spread(go)
        scores = nt(k, q_wide) * scale + bias_ref[grp]
        expo = jnp.exp(scores - jnp.max(scores, axis=0, keepdims=True))
        soft = expo * (1.0 / jnp.sum(expo, axis=0, keepdims=True))
        soft_b = soft.astype(bf16)
        gp = nt(v, go_wide)
        inner = jnp.sum(gp * soft, axis=0, keepdims=True)
        gs = (soft * (gp - inner) * scale).astype(bf16)
        heads[part, cq] = gather_heads(tn(soft_b, v)).astype(bf16)
        gproj[part, cq] = gather_heads(tn(gs, k)).astype(bf16)
        gproj[part, ck] = nn(gs, q_wide).astype(bf16)
        gproj[part, cv] = nn(soft_b, go_wide).astype(bf16)

    def attend_range(first, last, grp):
        def body(win, carry):
            attend(win, grp)
            return carry

        lax.fori_loop(first, last, body, 0)

    def weights(grp, half):
        lo = grp * GROUP

        def body(step, carry):
            rows = pl.ds(pl.multiple_of(half * 512 + step * 128, 128), 128)
            from_norm = jnp.concatenate([norm_t[t, rows, :] for t in range(4)], axis=1)
            from_g = jnp.concatenate([g_t[t, rows, :] for t in range(4)], axis=1)
            zs = pl.ds(step * 2, 2)
            for kind in range(3):
                cols = slice(kind * all_heads + lo, kind * all_heads + lo + GROUP)
                value = nn(from_norm, gproj[:, cols]).astype(bf16)
                m_ref[grp, half, zs, :, :, :, kind * GROUP:kind * GROUP + GROUP] = value.reshape(2, 2, 2, 16, GROUP)
            value = nn(from_g, heads[:, lo:lo + GROUP]).astype(bf16)
            m_ref[grp, half, zs, :, :, :, 3 * GROUP:] = value.reshape(2, 2, 2, 16, GROUP)
            return carry

        lax.fori_loop(0, nz // 2, body, 0)
        return send(m_ref.at[grp, half, :, :, 1 - core], recv0.at[grp, half], pair)

    def exchange(source, target, axis):
        return [send(source.at[on(axis, s)[0]], target.at[s - 1], on(axis, s)[1]) for s in range(1, size[axis])]

    def pair_add(index):
        order, grp, lo = PARTS[index]
        wide = 512 // nx

        def body(block, carry):
            a, b, c = block // (2 * nz), (block // 2) % nz, block % 2
            for part in range(nx):
                cols = slice(lo + part * wide, lo + part * wide + wide)
                at = {"x": part, "y": a * 2 + c, "z": b}
                acc1[index][at[order[0]], at[order[1]], at[order[2]]] = (
                    m_ref[grp, a, b, c, core, :, cols] + recv0[grp, a, b, c, :, cols])
            return carry

        lax.fori_loop(0, 4 * nz, body, 0)
        return exchange(acc1[index], rx1[index], order[0])

    def sum_one(index, arrivals):
        order = PARTS[index][0]
        landed(arrivals)
        mine = place[order[0]]

        def body(j, carry):
            for k in range(size[order[2]]):
                value = acc1[index][mine, j, k].astype(f32)
                for s in range(size[order[0]] - 1):
                    value = value + rx1[index][s, j, k].astype(f32)
                acc2[index][j, k] = value.astype(bf16)
            return carry

        lax.fori_loop(0, size[order[1]], body, 0)
        return exchange(acc2[index], rx2[index], order[1])

    def sum_two(index, arrivals):
        order = PARTS[index][0]
        landed(arrivals)
        mine = place[order[1]]
        for k in range(size[order[2]]):
            value = acc2[index][mine, k].astype(f32)
            for s in range(size[order[1]] - 1):
                value = value + rx2[index][s, k].astype(f32)
            acc3[index][k] = value.astype(bf16)
        return exchange(acc3[index], rx3[index], order[2])

    def sum_three(index, arrivals):
        order = PARTS[index][0]
        landed(arrivals)
        value = acc3[index][place[order[2]]].astype(f32)
        for s in range(size[order[2]] - 1):
            value = value + rx3[index][s].astype(f32)
        return value

    def finish(step):
        part = chunk(step)
        att = nn(heads[part, :], wout_ref[...]).astype(bf16)
        grad_normed = nt(gproj[part, :], wqkv_ref[...])
        inverse = inv_ref[part, :]
        unit = tok[0, 2 * step:2 * step + 2].reshape(128, 1024).astype(f32) * inverse
        grad_unit = grad_normed * gain_ref[...]
        mean = jnp.mean(grad_unit * unit, axis=1, keepdims=True)
        ret[0, 2 * step:2 * step + 2] = att.reshape(2, 4, 16, 1024)
        ret[1, 2 * step:2 * step + 2] = (inverse * (grad_unit - unit * mean)).astype(bf16).reshape(2, 4, 16, 1024)

    def residual(rb):
        for which, ref, target in ((0, img_ref, out_ref), (1, cot_ref, gimg_ref)):
            value = jnp.concatenate(
                [block_at(ret, back, which, block_place(rb, cb))[...] for cb in range(8)], axis=0)
            value = nn(from_block, value).reshape(4, 32, 1024)
            target[rb * 4:rb * 4 + 4] = (ref[rb * 4:rb * 4 + 4].astype(f32) + value).astype(bf16)

    for copy in copies:
        copy.wait()
    project(0)
    attend_range(0, 2, 0)
    landed(from_right)
    project(1)
    attend_range(2, 4, 0)
    landed(from_below)
    project(2)
    attend_range(4, 6, 0)
    landed(from_above)
    project(3)
    attend_range(6, 8, 0)
    paired0 = [weights(0, 0), weights(0, 1)]
    attend_range(0, 4, 1)
    landed(paired0)
    p0 = pair_add(0)
    p1 = pair_add(1)
    attend_range(4, 8, 1)
    paired1 = [weights(1, 0), weights(1, 1)]
    finish(2)
    b_above = [send(ret.at[:, 4:6, 2:4], b_up, below)]
    p1 = sum_one(1, p1)
    landed(paired1)
    p2 = pair_add(2)
    p3 = pair_add(3)
    finish(3)
    b_below = [
        send(ret.at[:, 6, 0], b_down.at[:, 0, 0], above),
        send(ret.at[:, 6, 1], b_down.at[:, 1, 0], above),
        send(ret.at[:, 7, 0], b_down.at[:, 2, 0], above),
    ]
    b_lefty = [
        send(ret.at[:, 7, 1], b_corner.at[:, 0, 0], above_right),
        send(ret.at[:, 7, 3], b_left.at[:, 0, 0], right),
    ]
    p0 = sum_one(0, p0)
    finish(1)
    b_lefty += [
        send(ret.at[:, 3, 1], b_left.at[:, 1, 0], right),
        send(ret.at[:, 3, 3], b_left.at[:, 2, 0], right),
    ]
    p1 = sum_two(1, p1)
    finish(0)
    p0 = sum_two(0, p0)
    p2 = sum_one(2, p2)
    p3 = sum_one(3, p3)
    landed(b_lefty)
    residual(1)
    residual(2)
    p2 = sum_two(2, p2)
    p3 = sum_two(3, p3)
    landed(b_above)
    residual(0)
    landed(b_below)
    residual(3)
    sums = [sum_three(0, p0), sum_three(1, p1), sum_three(2, p2), sum_three(3, p3)]
    near, far = jnp.concatenate(sums[0:2], axis=1), jnp.concatenate(sums[2:4], axis=1)
    for other in range(nx):
        swap_out[other, 0:4] = near[other * 4:other * 4 + 4]
        swap_out[other, 4:8] = far[other * 4:other * 4 + 4]
    last = exchange(swap_out, swap_in, "x")
    swap_in[nx - 1] = swap_out[x]
    landed(last)
    wide = 512 // nx
    for source in range(nx):
        got = swap_in[(x - source + nx - 1) % nx] * factor
        for index in range(count_parts):
            grp, lo = PARTS[index][1:]
            value = got[(index // 2) * 4:(index // 2) * 4 + 4, (index % 2) * wide:(index % 2) * wide + wide]
            kind, within = divmod(lo + source * wide, GROUP)
            if kind < 3:
                start = kind * all_heads + grp * GROUP + within
                gqkv_ref[:, start:start + wide] = value
            else:
                start = grp * GROUP + within
                gout_ref[:, start:start + wide] = value
    block = yh * (4 * nz) + z * 4 + yl * 2 + core
    own_rows = wqkv_ref[pl.ds(pl.multiple_of(block * 16, 16), 16), :].astype(f32)
    own = own_rows[0:4]
    for other in range(1, nx):
        own = jnp.where(x == other, own_rows[other * 4:other * 4 + 4], own)
    ggain_ref[...] = jnp.broadcast_to(jnp.sum(own * gqkv_ref[...], axis=1, keepdims=True), (4, 128))
    for copy in started:
        copy.wait_send()


def block(image, cotangent, gain, w_qkv, w_out, bias_table, nz, nx, factor):
    f32, bf16 = jnp.float32, jnp.bfloat16
    features = image.shape[-1]
    table = jnp.pad(bias_table, ((0, 0), (0, 1), (0, 1))).reshape(8, 256)
    size = {"x": nx, "y": 4, "z": nz}
    wide = 512 // nx
    orders = [part[0] for part in PARTS]
    dims = [[size[axis] for axis in order] for order in orders]
    shapes = [
        (w_qkv.shape, bf16), (w_out.shape, bf16),
        ((2, 8, 4, 16, features), bf16), ((2, 8, 4, 16, features), bf16),
    ]
    for _ in range(2):
        shapes += [((2, 2, 2, 16, features), bf16), ((2, 3, 1, 16, features), bf16),
                   ((2, 3, 1, 16, features), bf16), ((2, 1, 1, 16, features), bf16)]
    shapes += [
        ((4, features, 128), bf16), ((4, features, 128), bf16), ((512, 1), f32),
        ((512, 1536), bf16), ((512, 512), bf16), ((512, 512), bf16), ((512, 1536), bf16), ((2, 64, 256), f32),
        ((2, 2, nz, 2, 2, 16, 1024), bf16), ((2, 2, nz, 2, 16, 1024), bf16),
    ]
    shapes += [((a, b, c, 16, wide), bf16) for a, b, c in dims]
    shapes += [((b, c, 16, wide), bf16) for a, b, c in dims]
    shapes += [((c, 16, wide), bf16) for a, b, c in dims]
    shapes += [((a - 1, b, c, 16, wide), bf16) for a, b, c in dims]
    shapes += [((b - 1, c, 16, wide), bf16) for a, b, c in dims]
    shapes += [((c - 1, 16, wide), bf16) for a, b, c in dims]
    shapes += [((nx, 8, 2 * wide), f32), ((nx, 8, 2 * wide), f32)]
    count = 8 + 4 + 8 + len(PARTS) * (nx + nz + 4 - 3) + nx - 1
    vmem, hbm = pl.BlockSpec(memory_space=pltpu.VMEM), pl.BlockSpec(memory_space=pl.ANY)
    return pl.pallas_call(
        functools.partial(kernel, nz, nx, factor),
        out_shape=(
            jax.ShapeDtypeStruct(image.shape, bf16), jax.ShapeDtypeStruct(image.shape, bf16),
            jax.ShapeDtypeStruct((4, 1536), f32), jax.ShapeDtypeStruct((4, 512), f32),
            jax.ShapeDtypeStruct((4, 128), f32),
        ),
        in_specs=[vmem, vmem, vmem, hbm, hbm, vmem],
        out_specs=(vmem,) * 5,
        scratch_shapes=[pltpu.VMEM(shape, kind) for shape, kind in shapes]
        + [pltpu.SemaphoreType.DMA((count,)), pltpu.SemaphoreType.DMA((count,)), pltpu.SemaphoreType.DMA((2,))],
        compiler_params=pltpu.CompilerParams(
            collective_id=0, has_side_effects=True, vmem_limit_bytes=56 * 1024 * 1024),
        name="window_block",
    )(image, cotangent, gain.reshape(1, features), w_qkv, w_out, table)


def local(image, cotangent, gain, w_qkv, w_out, bias_table):
    total_count = (
        lax.axis_size("rows")
        * lax.axis_size("cols")
        * lax.axis_size("rep")
        * image.shape[1]
        * image.shape[2]
    )
    factor = 1.0 / float(np.sqrt(total_count))
    result, grad_result, grad_qkv, grad_out, gain_sum = block(
        image[0], cotangent[0], gain, w_qkv, w_out, bias_table,
        lax.axis_size("rows") // 2, lax.axis_size("rep"), factor)
    first = 4 * ((lax.axis_index("rows") * 4 + lax.axis_index("cols")) * 4 + lax.axis_index("rep"))
    own_gain = lax.dynamic_slice_in_dim(gain, first, 4, 0)
    return (result[None], grad_result[None], grad_qkv, grad_out.T, gain_sum[:, 0] / own_gain)


def solution(mesh):
    in_specs = (P("rep", "rows", "cols", None), P("rep", "rows", "cols", None), P(), P(), P(), P())
    out_specs = (
        P("rep", "rows", "cols", None),
        P("rep", "rows", "cols", None),
        P(("rows", "cols", "rep"), None),
        P(None, ("rows", "cols", "rep")),
        P(("rows", "cols", "rep")),
    )
    return jax.shard_map(local, mesh=mesh, in_specs=in_specs, out_specs=out_specs, check_vma=False)
```

```python
import functools

import jax
import jax.numpy as jnp
import numpy as np
from jax import lax
from jax.experimental import pallas as pl
from jax.experimental.pallas import tpu as pltpu
from jax.sharding import PartitionSpec as P

MESH = pl.DeviceIdType.MESH
EPS = 1e-06
GROUP = 256
HEAD = 64
PARTS = (("yxz", 0, 0), ("xyz", 0, 512), ("yxz", 1, 0), ("xyz", 1, 512))


def token_place(index):
    return (index // 32) * 4 + (index % 16) // 4, ((index // 16) % 2) * 4 + index % 4


def nt(left, right):
    return lax.dot_general(left, right, (((1,), (1,)), ((), ())), preferred_element_type=jnp.float32)


def tn(left, right):
    return lax.dot_general(left, right, (((0,), (0,)), ((), ())), preferred_element_type=jnp.float32)


def nn(left, right):
    return jnp.dot(left, right, preferred_element_type=jnp.float32)


def block_place(rb, cb):
    if cb == 0:
        return ("corner", 0, 0) if rb == 3 else ("left", rb, 0)
    if rb in (1, 2):
        return ("window", 3, (rb - 1) * 2) if cb == 7 else ("window", (cb - 1) // 2, (rb - 1) * 2 + (cb - 1) % 2)
    if rb == 3:
        return ("window", 4 + (cb - 1) // 2, (cb - 1) % 2) if cb <= 4 else ("down", cb - 5, 0)
    if cb <= 4:
        return ("up", (cb - 1) // 2, (cb - 1) % 2)
    return ("window", 7, 2) if cb == 7 else ("window", 6, 2 + cb - 5)


def kernel(nz, nx, factor,
           img_ref, cot_ref, gain_ref, wqkv_hbm, wout_hbm, table3_ref,
           att_ref, gtok_ref, gqkv_ref, gout_ref, ggain_ref,
           wqkv_ref, wout_ref, tok, ret,
           up, down, left, corner, b_up, b_down, b_left, b_corner,
           norm_t, g_t, inv_ref, proj, gheads, heads, gproj, bias_ref, table_ref,
           m_ref, recv0, *rest):
    f32, bf16, i32 = jnp.float32, jnp.bfloat16, jnp.int32
    count_parts = len(PARTS)
    acc1, acc2, acc3 = rest[0:4], rest[4:8], rest[8:12]
    rx1, rx2, rx3 = rest[12:16], rest[16:20], rest[20:24]
    sends, recvs, local_sems = rest[24:]
    scale = HEAD ** -0.5
    all_heads = 2 * GROUP

    row, col, x = lax.axis_index("rows"), lax.axis_index("cols"), lax.axis_index("rep")
    yh, z = row // nz, row % nz
    yl, core = col // 2, col % 2
    y = yh * 2 + yl
    place = {"x": x, "y": y, "z": z}
    size = {"x": nx, "y": 4, "z": nz}
    pair = (row, yl * 2 + 1 - core, x)
    above = ((row + 2 * nz - 1) % (2 * nz), col, x)
    below = ((row + 1) % (2 * nz), col, x)
    lefty = (row, (col + 3) % 4, x)
    right = (row, (col + 1) % 4, x)
    below_left = ((row + 1) % (2 * nz), (col + 3) % 4, x)
    above_right = ((row + 2 * nz - 1) % (2 * nz), (col + 1) % 4, x)

    def on(axis, step):
        other = (place[axis] + step) % size[axis]
        if axis == "x":
            return other, (row, col, other)
        if axis == "y":
            return other, ((other // 2) * nz + z, (other % 2) * 2 + core, x)
        return other, (yh * nz + other, col, x)

    copies = [
        pltpu.make_async_copy(wqkv_hbm, wqkv_ref, local_sems.at[0]),
        pltpu.make_async_copy(wout_hbm, wout_ref, local_sems.at[1]),
    ]
    for copy in copies:
        copy.start()

    barrier = pltpu.get_barrier_semaphore()
    peers = [pair, above, below, lefty, right, below_left, above_right]
    for axis in "xyz":
        peers += [on(axis, step)[1] for step in range(1, size[axis])]
    for peer in peers:
        pl.semaphore_signal(barrier, inc=1, device_id=peer, device_id_type=MESH)

    slot = iter(range(1000))
    started = []

    def send(source, target, device):
        index = next(slot)
        copy = pltpu.make_async_remote_copy(
            src_ref=source, dst_ref=target, send_sem=sends.at[index], recv_sem=recvs.at[index],
            device_id=device, device_id_type=MESH)
        copy.start()
        started.append(copy)
        return copy

    def landed(arrivals):
        for copy in arrivals:
            copy.wait_recv()

    rim = {"up": up, "down": down, "left": left, "corner": corner}
    back = {"up": b_up, "down": b_down, "left": b_left, "corner": b_corner}
    one = lax.broadcasted_iota(i32, (128, 128), 0)
    two = lax.broadcasted_iota(i32, (128, 128), 1)
    to_block = (two == ((one % 16) // 4) * 32 + (one // 16) * 4 + one % 4).astype(bf16)
    from_block = (two == ((one % 32) // 4) * 16 + (one // 32) * 4 + one % 4).astype(bf16)

    def block_at(own, rims, which, spot):
        name, a, b = spot
        if name == "window":
            return own.at[which, a, b]
        return rims[name].at[which, a, b]

    for rb in (0, 3, 1, 2):
        for which, ref in ((0, img_ref), (1, cot_ref)):
            value = nn(to_block, ref[rb * 4:rb * 4 + 4].reshape(128, 1024)).astype(bf16)
            for cb in range(8):
                block_at(tok, rim, which, block_place(rb, cb))[...] = value[cb * 16:cb * 16 + 16]

    pl.semaphore_wait(barrier, len(peers))
    from_right = [
        send(left.at[:, 1, 0], tok.at[:, 3, 1], lefty),
        send(left.at[:, 2, 0], tok.at[:, 3, 3], lefty),
    ]
    from_below = [send(up, tok.at[:, 4:6, 2:4], above)]
    from_above = [
        send(down.at[:, 0, 0], tok.at[:, 6, 0], below),
        send(down.at[:, 1, 0], tok.at[:, 6, 1], below),
        send(down.at[:, 2, 0], tok.at[:, 7, 0], below),
        send(corner.at[:, 0, 0], tok.at[:, 7, 1], below_left),
        send(left.at[:, 0, 0], tok.at[:, 7, 3], lefty),
    ]

    krow, kcol = token_place(lax.broadcasted_iota(i32, (64, 128), 0))
    qrow, qcol = token_place(lax.broadcasted_iota(i32, (64, 128), 1) % 64)
    offset = (qrow - krow + 7) * 16 + qcol - kcol + 7
    low, low_half = offset % 128, offset < 128
    first_head = lax.broadcasted_iota(i32, (64, 128), 1) < 64

    for dr in range(15):
        table_ref[:, dr * 16:dr * 16 + 15] = table3_ref[dr]

    def bias_of(head):
        at = functools.partial(jnp.take_along_axis, indices=low, axis=1, mode="promise_in_bounds")
        one_half = at(jnp.broadcast_to(table_ref[head:head + 1, 0:128], (64, 128)))
        return jnp.where(low_half, one_half, at(jnp.broadcast_to(table_ref[head:head + 1, 128:256], (64, 128))))

    for duo in range(4):
        bias_ref[duo // 2, :, (duo % 2) * 128:(duo % 2) * 128 + 128] = jnp.where(
            first_head, bias_of(2 * duo), bias_of(2 * duo + 1))

    def chunk(step):
        return slice(step * 128, step * 128 + 128)

    def project(step):
        part = chunk(step)
        value = tok[0, 2 * step:2 * step + 2].reshape(128, 1024).astype(f32)
        inverse = lax.rsqrt(jnp.mean(value * value, axis=1, keepdims=True) + EPS)
        inv_ref[part, :] = inverse
        normed = (value * inverse * gain_ref[...]).astype(bf16)
        upstream = tok[1, 2 * step:2 * step + 2].reshape(128, 1024)
        norm_t[step] = normed.T
        g_t[step] = upstream.T
        proj[part, :] = nn(normed, wqkv_ref[...]).astype(bf16)
        gheads[part, :] = nt(upstream, wout_ref[...]).astype(bf16)

    head_row = lax.broadcasted_iota(i32, (GROUP, GROUP), 0) // HEAD
    head_lane = lax.broadcasted_iota(i32, (GROUP, GROUP), 1) // HEAD
    diagonal = head_row == head_lane
    lane64 = lax.broadcasted_iota(i32, (64, GROUP), 1) // HEAD

    def spread(value):
        return jnp.where(diagonal, jnp.concatenate([value] * 4, axis=0), jnp.zeros((), value.dtype))

    def gather_heads(full):
        out = full[0:64]
        for h in range(1, 4):
            out = jnp.where(lane64 == h, full[h * 64:h * 64 + 64], out)
        return out

    def attend(win, grp):
        part = pl.ds(pl.multiple_of(win * 64, 64), 64)
        lo = grp * GROUP
        cq = slice(lo, lo + GROUP)
        ck = slice(all_heads + lo, all_heads + lo + GROUP)
        cv = slice(2 * all_heads + lo, 2 * all_heads + lo + GROUP)
        q, k, v, go = proj[part, cq], proj[part, ck], proj[part, cv], gheads[part, cq]
        q_wide, go_wide = spread(q), spread(go)
        scores = nt(k, q_wide) * scale + bias_ref[grp]
        expo = jnp.exp(scores - jnp.max(scores, axis=0, keepdims=True))
        soft = expo * (1.0 / jnp.sum(expo, axis=0, keepdims=True))
        soft_b = soft.astype(bf16)
        gp = nt(v, go_wide)
        inner = jnp.sum(gp * soft, axis=0, keepdims=True)
        gs = (soft * (gp - inner) * scale).astype(bf16)
        heads[part, cq] = gather_heads(tn(soft_b, v)).astype(bf16)
        gproj[part, cq] = gather_heads(tn(gs, k)).astype(bf16)
        gproj[part, ck] = nn(gs, q_wide).astype(bf16)
        gproj[part, cv] = nn(soft_b, go_wide).astype(bf16)

    def attend_range(first, last, grp):
        def body(win, carry):
            attend(win, grp)
            return carry

        lax.fori_loop(first, last, body, 0)

    def weights(grp, half):
        lo = grp * GROUP

        def body(step, carry):
            rows = pl.ds(pl.multiple_of(half * 512 + step * 128, 128), 128)
            from_norm = jnp.concatenate([norm_t[t, rows, :] for t in range(4)], axis=1)
            from_g = jnp.concatenate([g_t[t, rows, :] for t in range(4)], axis=1)
            zs = pl.ds(step * 2, 2)
            for kind in range(3):
                cols = slice(kind * all_heads + lo, kind * all_heads + lo + GROUP)
                value = nn(from_norm, gproj[:, cols]).astype(bf16)
                m_ref[grp, half, zs, :, :, :, kind * GROUP:kind * GROUP + GROUP] = value.reshape(2, 2, 2, 16, GROUP)
            value = nn(from_g, heads[:, lo:lo + GROUP]).astype(bf16)
            m_ref[grp, half, zs, :, :, :, 3 * GROUP:] = value.reshape(2, 2, 2, 16, GROUP)
            return carry

        lax.fori_loop(0, nz // 2, body, 0)
        return send(m_ref.at[grp, half, :, :, 1 - core], recv0.at[grp, half], pair)

    def exchange(source, target, axis):
        return [send(source.at[on(axis, s)[0]], target.at[s - 1], on(axis, s)[1]) for s in range(1, size[axis])]

    def pair_add(index):
        order, grp, lo = PARTS[index]

        def body(block, carry):
            a, b, c = block // (2 * nz), (block // 2) % nz, block % 2
            cols = slice(lo, lo + 512)
            value = m_ref[grp, a, b, c, core, :, cols].astype(f32) + recv0[grp, a, b, c, :, cols].astype(f32)
            for part in range(nx):
                rows = value[part * 4:part * 4 + 4]
                tile = jnp.concatenate([rows[:, j * 128:j * 128 + 128] for j in range(4)], axis=0)
                at = {"x": part, "y": a * 2 + c, "z": b}
                acc1[index][at[order[0]], at[order[1]], at[order[2]]] = tile.astype(bf16)
            return carry

        lax.fori_loop(0, 4 * nz, body, 0)
        return exchange(acc1[index], rx1[index], order[0])

    def sum_one(index, arrivals):
        order = PARTS[index][0]
        landed(arrivals)
        mine = place[order[0]]

        def body(j, carry):
            for k in range(size[order[2]]):
                value = acc1[index][mine, j, k].astype(f32)
                for s in range(size[order[0]] - 1):
                    value = value + rx1[index][s, j, k].astype(f32)
                acc2[index][j, k] = value.astype(bf16)
            return carry

        lax.fori_loop(0, size[order[1]], body, 0)
        return exchange(acc2[index], rx2[index], order[1])

    def sum_two(index, arrivals):
        order = PARTS[index][0]
        landed(arrivals)
        mine = place[order[1]]
        for k in range(size[order[2]]):
            value = acc2[index][mine, k].astype(f32)
            for s in range(size[order[1]] - 1):
                value = value + rx2[index][s, k].astype(f32)
            acc3[index][k] = value.astype(bf16)
        return exchange(acc3[index], rx3[index], order[2])

    def sum_three(index, arrivals):
        order = PARTS[index][0]
        landed(arrivals)
        value = acc3[index][place[order[2]]].astype(f32)
        for s in range(size[order[2]] - 1):
            value = value + rx3[index][s].astype(f32)
        return value

    def finish(step):
        part = chunk(step)
        att = nn(heads[part, :], wout_ref[...]).astype(bf16)
        grad_normed = nt(gproj[part, :], wqkv_ref[...])
        inverse = inv_ref[part, :]
        unit = tok[0, 2 * step:2 * step + 2].reshape(128, 1024).astype(f32) * inverse
        grad_unit = grad_normed * gain_ref[...]
        mean = jnp.mean(grad_unit * unit, axis=1, keepdims=True)
        ret[0, 2 * step:2 * step + 2] = att.reshape(2, 4, 16, 1024)
        ret[1, 2 * step:2 * step + 2] = (inverse * (grad_unit - unit * mean)).astype(bf16).reshape(2, 4, 16, 1024)

    def residual(rb):
        for which, target in ((0, att_ref), (1, gtok_ref)):
            value = jnp.concatenate(
                [block_at(ret, back, which, block_place(rb, cb))[...] for cb in range(8)], axis=0)
            target[rb * 4:rb * 4 + 4] = nn(from_block, value).astype(bf16).reshape(4, 32, 1024)

    for copy in copies:
        copy.wait()
    project(0)
    attend_range(0, 2, 0)
    landed(from_right)
    project(1)
    attend_range(2, 4, 0)
    attend_range(0, 4, 1)
    landed(from_below)
    project(2)
    attend_range(4, 6, 0)
    landed(from_above)
    project(3)
    attend_range(6, 8, 0)
    paired0 = [weights(0, 0), weights(0, 1)]
    attend_range(4, 6, 1)
    landed(paired0)
    p0 = pair_add(0)
    p1 = pair_add(1)
    attend_range(6, 8, 1)
    paired1 = [weights(1, 0), weights(1, 1)]
    finish(2)
    b_above = [send(ret.at[:, 4:6, 2:4], b_up, below)]
    landed(paired1)
    p2 = pair_add(2)
    p3 = pair_add(3)
    finish(3)
    b_below = [
        send(ret.at[:, 6, 0], b_down.at[:, 0, 0], above),
        send(ret.at[:, 6, 1], b_down.at[:, 1, 0], above),
        send(ret.at[:, 7, 0], b_down.at[:, 2, 0], above),
    ]
    b_lefty = [
        send(ret.at[:, 7, 1], b_corner.at[:, 0, 0], above_right),
        send(ret.at[:, 7, 3], b_left.at[:, 0, 0], right),
    ]
    p0 = sum_one(0, p0)
    p1 = sum_one(1, p1)
    finish(1)
    b_lefty += [
        send(ret.at[:, 3, 1], b_left.at[:, 1, 0], right),
        send(ret.at[:, 3, 3], b_left.at[:, 2, 0], right),
    ]
    finish(0)
    p0 = sum_two(0, p0)
    p1 = sum_two(1, p1)
    p2 = sum_one(2, p2)
    p3 = sum_one(3, p3)
    landed(b_lefty)
    residual(1)
    residual(2)
    p2 = sum_two(2, p2)
    p3 = sum_two(3, p3)
    landed(b_above)
    residual(0)
    landed(b_below)
    residual(3)
    arrivals = [p0, p1, p2, p3]
    for index in range(count_parts):
        grp, lo = PARTS[index][1:]
        got = sum_three(index, arrivals[index]) * factor
        for j in range(4):
            kind, within = divmod(lo + j * 128, GROUP)
            start = grp * GROUP + within
            if kind < 3:
                start += kind * all_heads
                gqkv_ref[:, start:start + 128] = got[j * 4:j * 4 + 4]
            else:
                gout_ref[:, start:start + 128] = got[j * 4:j * 4 + 4]
    block = yh * (4 * nz) + z * 4 + yl * 2 + core
    own_rows = wqkv_ref[pl.ds(pl.multiple_of(block * 16, 16), 16), :].astype(f32)
    own = own_rows[0:4]
    for other in range(1, nx):
        own = jnp.where(x == other, own_rows[other * 4:other * 4 + 4], own)
    lane = lax.broadcasted_iota(i32, (4, 1024), 1)
    mine = lane == (block * nx + x) * 4 + lax.broadcasted_iota(i32, (4, 1024), 0)
    own_gain = jnp.sum(jnp.where(mine, gain_ref[...], 0.0), axis=1, keepdims=True)
    value = jnp.sum(own * gqkv_ref[...], axis=1, keepdims=True) / own_gain
    spot = lax.broadcasted_iota(i32, (4, 128), 0) == lax.broadcasted_iota(i32, (4, 128), 1)
    ggain_ref[...] = jnp.sum(jnp.where(spot, value, 0.0), axis=0, keepdims=True)[:, 0:4]
    for copy in started:
        copy.wait_send()


def block(image, cotangent, gain, w_qkv, w_out, bias_table, nz, nx, factor):
    f32, bf16 = jnp.float32, jnp.bfloat16
    features = image.shape[-1]
    table = bias_table.transpose(1, 0, 2)
    size = {"x": nx, "y": 4, "z": nz}
    wide = 128
    orders = [part[0] for part in PARTS]
    dims = [[size[axis] for axis in order] for order in orders]
    shapes = [
        (w_qkv.shape, bf16), (w_out.shape, bf16),
        ((2, 8, 4, 16, features), bf16), ((2, 8, 4, 16, features), bf16),
    ]
    for _ in range(2):
        shapes += [((2, 2, 2, 16, features), bf16), ((2, 3, 1, 16, features), bf16),
                   ((2, 3, 1, 16, features), bf16), ((2, 1, 1, 16, features), bf16)]
    shapes += [
        ((4, features, 128), bf16), ((4, features, 128), bf16), ((512, 1), f32),
        ((512, 1536), bf16), ((512, 512), bf16), ((512, 512), bf16), ((512, 1536), bf16), ((2, 64, 256), f32), ((8, 256), f32),
        ((2, 2, nz, 2, 2, 16, 1024), bf16), ((2, 2, nz, 2, 16, 1024), bf16),
    ]
    shapes += [((a, b, c, 16, wide), bf16) for a, b, c in dims]
    shapes += [((b, c, 16, wide), bf16) for a, b, c in dims]
    shapes += [((c, 16, wide), bf16) for a, b, c in dims]
    shapes += [((a - 1, b, c, 16, wide), bf16) for a, b, c in dims]
    shapes += [((b - 1, c, 16, wide), bf16) for a, b, c in dims]
    shapes += [((c - 1, 16, wide), bf16) for a, b, c in dims]
    count = 8 + 4 + 8 + len(PARTS) * (nx + nz + 4 - 3)
    vmem, hbm = pl.BlockSpec(memory_space=pltpu.VMEM), pl.BlockSpec(memory_space=pl.ANY)
    return pl.pallas_call(
        functools.partial(kernel, nz, nx, factor),
        out_shape=(
            jax.ShapeDtypeStruct(image.shape, bf16), jax.ShapeDtypeStruct(image.shape, bf16),
            jax.ShapeDtypeStruct((4, 1536), f32), jax.ShapeDtypeStruct((4, 512), f32),
            jax.ShapeDtypeStruct((1, 4), f32),
        ),
        in_specs=[vmem, vmem, vmem, hbm, hbm, vmem],
        out_specs=(vmem,) * 5,
        scratch_shapes=[pltpu.VMEM(shape, kind) for shape, kind in shapes]
        + [pltpu.SemaphoreType.DMA((count,)), pltpu.SemaphoreType.DMA((count,)), pltpu.SemaphoreType.DMA((2,))],
        compiler_params=pltpu.CompilerParams(
            collective_id=0, has_side_effects=True, vmem_limit_bytes=56 * 1024 * 1024),
        name="window_block",
    )(image, cotangent, gain.reshape(1, features), w_qkv, w_out, table)


def add_kernel(img_ref, cot_ref, att_ref, gtok_ref, gqkv_in, gout_in, ggain_in,
               out_ref, gimg_ref, gqkv_ref, gout_ref, ggain_ref):
    f32, bf16 = jnp.float32, jnp.bfloat16
    out_ref[...] = (img_ref[...].astype(f32) + att_ref[...].astype(f32)).astype(bf16)
    gimg_ref[...] = (cot_ref[...].astype(f32) + gtok_ref[...].astype(f32)).astype(bf16)
    gqkv_ref[...] = gqkv_in[...]
    gout_ref[...] = gout_in[...]
    ggain_ref[...] = ggain_in[...]


def add_branches(image, cotangent, attention, grad_tokens, grad_qkv, grad_out, grad_gain):
    rows, cols, features = image.shape
    steps = 4
    tile = pl.BlockSpec((rows // steps, cols, features), lambda i: (i, 0, 0))
    small = [pl.BlockSpec(value.shape, lambda i: (0, 0)) for value in (grad_qkv, grad_out, grad_gain)]
    return pl.pallas_call(
        add_kernel,
        grid=(steps,),
        out_shape=(
            jax.ShapeDtypeStruct(image.shape, image.dtype), jax.ShapeDtypeStruct(image.shape, image.dtype),
            jax.ShapeDtypeStruct(grad_qkv.shape, jnp.float32), jax.ShapeDtypeStruct(grad_out.shape, jnp.float32),
            jax.ShapeDtypeStruct(grad_gain.shape, jnp.float32),
        ),
        in_specs=[tile] * 4 + small,
        out_specs=(tile, tile, *small),
        name="add_branches",
    )(image, cotangent, attention, grad_tokens, grad_qkv, grad_out, grad_gain)


def local(image, cotangent, gain, w_qkv, w_out, bias_table):
    total_count = (
        lax.axis_size("rows")
        * lax.axis_size("cols")
        * lax.axis_size("rep")
        * image.shape[1]
        * image.shape[2]
    )
    factor = 1.0 / float(np.sqrt(total_count))
    branches = block(
        image[0], cotangent[0], gain, w_qkv, w_out, bias_table,
        lax.axis_size("rows") // 2, lax.axis_size("rep"), factor)
    result, grad_result, grad_qkv, grad_out, grad_gain = add_branches(image[0], cotangent[0], *branches)
    return (result[None], grad_result[None], grad_qkv, grad_out.T, grad_gain.reshape(4))


def solution(mesh):
    in_specs = (P("rep", "rows", "cols", None), P("rep", "rows", "cols", None), P(), P(), P(), P())
    out_specs = (
        P("rep", "rows", "cols", None),
        P("rep", "rows", "cols", None),
        P(("rows", "cols", "rep"), None),
        P(None, ("rows", "cols", "rep")),
        P(("rows", "cols", "rep")),
    )
    return jax.shard_map(local, mesh=mesh, in_specs=in_specs, out_specs=out_specs, check_vma=False)
```

```python
import functools

import jax
import jax.numpy as jnp
import numpy as np
from jax import lax
from jax.experimental import pallas as pl
from jax.experimental.pallas import tpu as pltpu
from jax.sharding import PartitionSpec as P

MESH = pl.DeviceIdType.MESH
EPS = 1e-06
GROUP = 256
HEAD = 64
PARTS = (("yxz", 0, 0), ("xyz", 0, 512), ("yxz", 1, 0), ("xyz", 1, 512))


def token_place(index):
    return (index // 32) * 4 + (index % 16) // 4, ((index // 16) % 2) * 4 + index % 4


def nt(left, right):
    return lax.dot_general(left, right, (((1,), (1,)), ((), ())), preferred_element_type=jnp.float32)


def tn(left, right):
    return lax.dot_general(left, right, (((0,), (0,)), ((), ())), preferred_element_type=jnp.float32)


def nn(left, right):
    return jnp.dot(left, right, preferred_element_type=jnp.float32)


def block_place(rb, cb):
    if cb == 0:
        return ("corner", 0, 0) if rb == 3 else ("left", rb, 0)
    if rb in (1, 2):
        return ("window", 3, (rb - 1) * 2) if cb == 7 else ("window", (cb - 1) // 2, (rb - 1) * 2 + (cb - 1) % 2)
    if rb == 3:
        return ("window", 4 + (cb - 1) // 2, (cb - 1) % 2) if cb <= 4 else ("down", cb - 5, 0)
    if cb <= 4:
        return ("up", (cb - 1) // 2, (cb - 1) % 2)
    return ("window", 7, 2) if cb == 7 else ("window", 6, 2 + cb - 5)


def kernel(nz, nx, factor,
           img_ref, cot_ref, gain_ref, wqkv_hbm, wout_hbm, table3_ref,
           att_ref, gtok_ref, gqkv_ref, gout_ref, ggain_ref,
           wqkv_ref, wout_ref, tok, ret,
           up, down, left, corner, b_up, b_down, b_left, b_corner,
           norm_t, g_t, inv_ref, proj, gheads, heads, gproj, bias_ref, table_ref,
           m_ref, recv0, *rest):
    f32, bf16, i32 = jnp.float32, jnp.bfloat16, jnp.int32
    count_parts = len(PARTS)
    acc1, acc2, acc3 = rest[0:4], rest[4:8], rest[8:12]
    rx1, rx2, rx3 = rest[12:16], rest[16:20], rest[20:24]
    sends, recvs, local_sems = rest[24:]
    scale = HEAD ** -0.5
    all_heads = 2 * GROUP

    row, col, x = lax.axis_index("rows"), lax.axis_index("cols"), lax.axis_index("rep")
    yh, z = row // nz, row % nz
    yl, core = col // 2, col % 2
    y = yh * 2 + yl
    place = {"x": x, "y": y, "z": z}
    size = {"x": nx, "y": 4, "z": nz}
    pair = (row, yl * 2 + 1 - core, x)
    above = ((row + 2 * nz - 1) % (2 * nz), col, x)
    below = ((row + 1) % (2 * nz), col, x)
    lefty = (row, (col + 3) % 4, x)
    right = (row, (col + 1) % 4, x)
    below_left = ((row + 1) % (2 * nz), (col + 3) % 4, x)
    above_right = ((row + 2 * nz - 1) % (2 * nz), (col + 1) % 4, x)

    def on(axis, step):
        other = (place[axis] + step) % size[axis]
        if axis == "x":
            return other, (row, col, other)
        if axis == "y":
            return other, ((other // 2) * nz + z, (other % 2) * 2 + core, x)
        return other, (yh * nz + other, col, x)

    copies = [
        pltpu.make_async_copy(wqkv_hbm, wqkv_ref, local_sems.at[0]),
        pltpu.make_async_copy(wout_hbm, wout_ref, local_sems.at[1]),
    ]
    for copy in copies:
        copy.start()

    barrier = pltpu.get_barrier_semaphore()
    peers = [pair, above, below, lefty, right, below_left, above_right]
    for axis in "xyz":
        peers += [on(axis, step)[1] for step in range(1, size[axis])]
    for peer in peers:
        pl.semaphore_signal(barrier, inc=1, device_id=peer, device_id_type=MESH)

    slot = iter(range(1000))
    started = []

    def send(source, target, device):
        index = next(slot)
        copy = pltpu.make_async_remote_copy(
            src_ref=source, dst_ref=target, send_sem=sends.at[index], recv_sem=recvs.at[index],
            device_id=device, device_id_type=MESH)
        copy.start()
        started.append(copy)
        return copy

    def landed(arrivals):
        for copy in arrivals:
            copy.wait_recv()

    rim = {"up": up, "down": down, "left": left, "corner": corner}
    back = {"up": b_up, "down": b_down, "left": b_left, "corner": b_corner}
    one = lax.broadcasted_iota(i32, (128, 128), 0)
    two = lax.broadcasted_iota(i32, (128, 128), 1)
    to_block = (two == ((one % 16) // 4) * 32 + (one // 16) * 4 + one % 4).astype(bf16)
    from_block = (two == ((one % 32) // 4) * 16 + (one // 32) * 4 + one % 4).astype(bf16)

    def block_at(own, rims, which, spot):
        name, a, b = spot
        if name == "window":
            return own.at[which, a, b]
        return rims[name].at[which, a, b]

    for rb in (0, 3, 1, 2):
        for which, ref in ((0, img_ref), (1, cot_ref)):
            value = nn(to_block, ref[rb * 4:rb * 4 + 4].reshape(128, 1024)).astype(bf16)
            for cb in range(8):
                block_at(tok, rim, which, block_place(rb, cb))[...] = value[cb * 16:cb * 16 + 16]

    pl.semaphore_wait(barrier, len(peers))
    from_right = [
        send(left.at[:, 1, 0], tok.at[:, 3, 1], lefty),
        send(left.at[:, 2, 0], tok.at[:, 3, 3], lefty),
    ]
    from_below = [send(up, tok.at[:, 4:6, 2:4], above)]
    from_above = [
        send(down.at[:, 0, 0], tok.at[:, 6, 0], below),
        send(down.at[:, 1, 0], tok.at[:, 6, 1], below),
        send(down.at[:, 2, 0], tok.at[:, 7, 0], below),
        send(corner.at[:, 0, 0], tok.at[:, 7, 1], below_left),
        send(left.at[:, 0, 0], tok.at[:, 7, 3], lefty),
    ]

    krow, kcol = token_place(lax.broadcasted_iota(i32, (64, 128), 0))
    qrow, qcol = token_place(lax.broadcasted_iota(i32, (64, 128), 1) % 64)
    offset = (qrow - krow + 7) * 16 + qcol - kcol + 7
    low, low_half = offset % 128, offset < 128
    first_head = lax.broadcasted_iota(i32, (64, 128), 1) < 64

    for dr in range(15):
        table_ref[:, dr * 16:dr * 16 + 15] = table3_ref[dr]

    def bias_of(head):
        at = functools.partial(jnp.take_along_axis, indices=low, axis=1, mode="promise_in_bounds")
        one_half = at(jnp.broadcast_to(table_ref[head:head + 1, 0:128], (64, 128)))
        return jnp.where(low_half, one_half, at(jnp.broadcast_to(table_ref[head:head + 1, 128:256], (64, 128))))

    for duo in range(4):
        bias_ref[duo // 2, :, (duo % 2) * 128:(duo % 2) * 128 + 128] = jnp.where(
            first_head, bias_of(2 * duo), bias_of(2 * duo + 1))

    def chunk(step):
        return slice(step * 128, step * 128 + 128)

    def project(step):
        part = chunk(step)
        value = tok[0, 2 * step:2 * step + 2].reshape(128, 1024).astype(f32)
        inverse = lax.rsqrt(jnp.mean(value * value, axis=1, keepdims=True) + EPS)
        inv_ref[part, :] = inverse
        normed = (value * inverse * gain_ref[...]).astype(bf16)
        upstream = tok[1, 2 * step:2 * step + 2].reshape(128, 1024)
        norm_t[step] = normed.T
        g_t[step] = upstream.T
        proj[part, :] = nn(normed, wqkv_ref[...]).astype(bf16)
        gheads[part, :] = nt(upstream, wout_ref[...]).astype(bf16)

    head_row = lax.broadcasted_iota(i32, (GROUP, GROUP), 0) // HEAD
    head_lane = lax.broadcasted_iota(i32, (GROUP, GROUP), 1) // HEAD
    diagonal = head_row == head_lane
    lane64 = lax.broadcasted_iota(i32, (64, GROUP), 1) // HEAD

    def spread(value):
        return jnp.where(diagonal, jnp.concatenate([value] * 4, axis=0), jnp.zeros((), value.dtype))

    def gather_heads(full):
        out = full[0:64]
        for h in range(1, 4):
            out = jnp.where(lane64 == h, full[h * 64:h * 64 + 64], out)
        return out

    def attend(win, grp):
        part = pl.ds(pl.multiple_of(win * 64, 64), 64)
        lo = grp * GROUP
        cq = slice(lo, lo + GROUP)
        ck = slice(all_heads + lo, all_heads + lo + GROUP)
        cv = slice(2 * all_heads + lo, 2 * all_heads + lo + GROUP)
        q, k, v, go = proj[part, cq], proj[part, ck], proj[part, cv], gheads[part, cq]
        q_wide, go_wide = spread(q), spread(go)
        scores = nt(k, q_wide) * scale + bias_ref[grp]
        expo = jnp.exp(scores - jnp.max(scores, axis=0, keepdims=True))
        soft = expo * (1.0 / jnp.sum(expo, axis=0, keepdims=True))
        soft_b = soft.astype(bf16)
        gp = nt(v, go_wide)
        inner = jnp.sum(gp * soft, axis=0, keepdims=True)
        gs = (soft * (gp - inner) * scale).astype(bf16)
        heads[part, cq] = gather_heads(tn(soft_b, v)).astype(bf16)
        gproj[part, cq] = gather_heads(tn(gs, k)).astype(bf16)
        gproj[part, ck] = nn(gs, q_wide).astype(bf16)
        gproj[part, cv] = nn(soft_b, go_wide).astype(bf16)

    def attend_range(first, last, grp):
        def body(win, carry):
            attend(win, grp)
            return carry

        lax.fori_loop(first, last, body, 0)

    def weights(grp, half):
        lo = grp * GROUP

        def body(step, carry):
            rows = pl.ds(pl.multiple_of(half * 512 + step * 128, 128), 128)
            from_norm = jnp.concatenate([norm_t[t, rows, :] for t in range(4)], axis=1)
            from_g = jnp.concatenate([g_t[t, rows, :] for t in range(4)], axis=1)
            zs = pl.ds(step * 2, 2)
            for kind in range(3):
                cols = slice(kind * all_heads + lo, kind * all_heads + lo + GROUP)
                value = nn(from_norm, gproj[:, cols]).astype(bf16)
                m_ref[grp, half, zs, :, :, :, kind * GROUP:kind * GROUP + GROUP] = value.reshape(2, 2, 2, 16, GROUP)
            value = nn(from_g, heads[:, lo:lo + GROUP]).astype(bf16)
            m_ref[grp, half, zs, :, :, :, 3 * GROUP:] = value.reshape(2, 2, 2, 16, GROUP)
            return carry

        lax.fori_loop(0, nz // 2, body, 0)
        return send(m_ref.at[grp, half, :, :, 1 - core], recv0.at[grp, half], pair)

    def exchange(source, target, axis):
        return [send(source.at[on(axis, s)[0]], target.at[s - 1], on(axis, s)[1]) for s in range(1, size[axis])]

    def pair_add(index):
        order, grp, lo = PARTS[index]

        def body(block, carry):
            a, b, c = block // (2 * nz), (block // 2) % nz, block % 2
            cols = slice(lo, lo + 512)
            value = m_ref[grp, a, b, c, core, :, cols].astype(f32) + recv0[grp, a, b, c, :, cols].astype(f32)
            for part in range(nx):
                rows = value[part * 4:part * 4 + 4]
                tile = jnp.concatenate([rows[:, j * 128:j * 128 + 128] for j in range(4)], axis=0)
                at = {"x": part, "y": a * 2 + c, "z": b}
                acc1[index][at[order[0]], at[order[1]], at[order[2]]] = tile.astype(bf16)
            return carry

        lax.fori_loop(0, 4 * nz, body, 0)
        return exchange(acc1[index], rx1[index], order[0])

    def sum_one(index, arrivals):
        order = PARTS[index][0]
        landed(arrivals)
        mine = place[order[0]]

        def body(j, carry):
            for k in range(size[order[2]]):
                value = acc1[index][mine, j, k].astype(f32)
                for s in range(size[order[0]] - 1):
                    value = value + rx1[index][s, j, k].astype(f32)
                acc2[index][j, k] = value.astype(bf16)
            return carry

        lax.fori_loop(0, size[order[1]], body, 0)
        return exchange(acc2[index], rx2[index], order[1])

    def sum_two(index, arrivals):
        order = PARTS[index][0]
        landed(arrivals)
        mine = place[order[1]]
        for k in range(size[order[2]]):
            value = acc2[index][mine, k].astype(f32)
            for s in range(size[order[1]] - 1):
                value = value + rx2[index][s, k].astype(f32)
            acc3[index][k] = value.astype(bf16)
        return exchange(acc3[index], rx3[index], order[2])

    def sum_three(index, arrivals):
        order = PARTS[index][0]
        landed(arrivals)
        value = acc3[index][place[order[2]]].astype(f32)
        for s in range(size[order[2]] - 1):
            value = value + rx3[index][s].astype(f32)
        return value

    def finish(step):
        part = chunk(step)
        att = nn(heads[part, :], wout_ref[...]).astype(bf16)
        grad_normed = nt(gproj[part, :], wqkv_ref[...])
        inverse = inv_ref[part, :]
        unit = tok[0, 2 * step:2 * step + 2].reshape(128, 1024).astype(f32) * inverse
        grad_unit = grad_normed * gain_ref[...]
        mean = jnp.mean(grad_unit * unit, axis=1, keepdims=True)
        ret[0, 2 * step:2 * step + 2] = att.reshape(2, 4, 16, 1024)
        ret[1, 2 * step:2 * step + 2] = (inverse * (grad_unit - unit * mean)).astype(bf16).reshape(2, 4, 16, 1024)

    def residual(rb):
        for which, target in ((0, att_ref), (1, gtok_ref)):
            value = jnp.concatenate(
                [block_at(ret, back, which, block_place(rb, cb))[...] for cb in range(8)], axis=0)
            target[rb * 4:rb * 4 + 4] = nn(from_block, value).astype(bf16).reshape(4, 32, 1024)

    for copy in copies:
        copy.wait()
    project(0)
    attend_range(0, 2, 0)
    landed(from_right)
    project(1)
    attend_range(2, 4, 0)
    attend_range(0, 4, 1)
    landed(from_below)
    project(2)
    attend_range(4, 6, 0)
    landed(from_above)
    project(3)
    attend_range(6, 8, 0)
    paired0 = [weights(0, 0), weights(0, 1)]
    attend_range(4, 6, 1)
    landed(paired0)
    p0 = pair_add(0)
    p1 = pair_add(1)
    attend_range(6, 8, 1)
    paired1 = [weights(1, 0), weights(1, 1)]
    finish(2)
    landed(paired1)
    p2 = pair_add(2)
    p3 = pair_add(3)
    finish(3)
    p0 = sum_one(0, p0)
    p1 = sum_one(1, p1)
    finish(1)
    finish(0)
    p0 = sum_two(0, p0)
    p1 = sum_two(1, p1)
    p2 = sum_one(2, p2)
    p3 = sum_one(3, p3)
    b_above = [send(ret.at[:, 4:6, 2:4], b_up, below)]
    b_below = [
        send(ret.at[:, 6, 0], b_down.at[:, 0, 0], above),
        send(ret.at[:, 6, 1], b_down.at[:, 1, 0], above),
        send(ret.at[:, 7, 0], b_down.at[:, 2, 0], above),
    ]
    b_lefty = [
        send(ret.at[:, 7, 1], b_corner.at[:, 0, 0], above_right),
        send(ret.at[:, 7, 3], b_left.at[:, 0, 0], right),
    ]
    b_lefty += [
        send(ret.at[:, 3, 1], b_left.at[:, 1, 0], right),
        send(ret.at[:, 3, 3], b_left.at[:, 2, 0], right),
    ]
    p2 = sum_two(2, p2)
    p3 = sum_two(3, p3)
    landed(b_lefty)
    residual(1)
    residual(2)
    landed(b_above)
    residual(0)
    landed(b_below)
    residual(3)
    arrivals = [p0, p1, p2, p3]
    for index in range(count_parts):
        grp, lo = PARTS[index][1:]
        got = sum_three(index, arrivals[index]) * factor
        for j in range(4):
            kind, within = divmod(lo + j * 128, GROUP)
            start = grp * GROUP + within
            if kind < 3:
                start += kind * all_heads
                gqkv_ref[:, start:start + 128] = got[j * 4:j * 4 + 4]
            else:
                gout_ref[:, start:start + 128] = got[j * 4:j * 4 + 4]
    block = yh * (4 * nz) + z * 4 + yl * 2 + core
    own_rows = wqkv_ref[pl.ds(pl.multiple_of(block * 16, 16), 16), :].astype(f32)
    own = own_rows[0:4]
    for other in range(1, nx):
        own = jnp.where(x == other, own_rows[other * 4:other * 4 + 4], own)
    lane = lax.broadcasted_iota(i32, (4, 1024), 1)
    mine = lane == (block * nx + x) * 4 + lax.broadcasted_iota(i32, (4, 1024), 0)
    own_gain = jnp.sum(jnp.where(mine, gain_ref[...], 0.0), axis=1, keepdims=True)
    value = jnp.sum(own * gqkv_ref[...], axis=1, keepdims=True) / own_gain
    spot = lax.broadcasted_iota(i32, (4, 128), 0) == lax.broadcasted_iota(i32, (4, 128), 1)
    ggain_ref[...] = jnp.sum(jnp.where(spot, value, 0.0), axis=0, keepdims=True)[:, 0:4]
    for copy in started:
        copy.wait_send()


def block(image, cotangent, gain, w_qkv, w_out, bias_table, nz, nx, factor):
    f32, bf16 = jnp.float32, jnp.bfloat16
    features = image.shape[-1]
    table = bias_table.transpose(1, 0, 2)
    size = {"x": nx, "y": 4, "z": nz}
    wide = 128
    orders = [part[0] for part in PARTS]
    dims = [[size[axis] for axis in order] for order in orders]
    shapes = [
        (w_qkv.shape, bf16), (w_out.shape, bf16),
        ((2, 8, 4, 16, features), bf16), ((2, 8, 4, 16, features), bf16),
    ]
    for _ in range(2):
        shapes += [((2, 2, 2, 16, features), bf16), ((2, 3, 1, 16, features), bf16),
                   ((2, 3, 1, 16, features), bf16), ((2, 1, 1, 16, features), bf16)]
    shapes += [
        ((4, features, 128), bf16), ((4, features, 128), bf16), ((512, 1), f32),
        ((512, 1536), bf16), ((512, 512), bf16), ((512, 512), bf16), ((512, 1536), bf16), ((2, 64, 256), f32), ((8, 256), f32),
        ((2, 2, nz, 2, 2, 16, 1024), bf16), ((2, 2, nz, 2, 16, 1024), bf16),
    ]
    shapes += [((a, b, c, 16, wide), bf16) for a, b, c in dims]
    shapes += [((b, c, 16, wide), bf16) for a, b, c in dims]
    shapes += [((c, 16, wide), bf16) for a, b, c in dims]
    shapes += [((a - 1, b, c, 16, wide), bf16) for a, b, c in dims]
    shapes += [((b - 1, c, 16, wide), bf16) for a, b, c in dims]
    shapes += [((c - 1, 16, wide), bf16) for a, b, c in dims]
    count = 8 + 4 + 8 + len(PARTS) * (nx + nz + 4 - 3)
    vmem, hbm = pl.BlockSpec(memory_space=pltpu.VMEM), pl.BlockSpec(memory_space=pl.ANY)
    return pl.pallas_call(
        functools.partial(kernel, nz, nx, factor),
        out_shape=(
            jax.ShapeDtypeStruct(image.shape, bf16), jax.ShapeDtypeStruct(image.shape, bf16),
            jax.ShapeDtypeStruct((4, 1536), f32), jax.ShapeDtypeStruct((4, 512), f32),
            jax.ShapeDtypeStruct((1, 4), f32),
        ),
        in_specs=[vmem, vmem, vmem, hbm, hbm, vmem],
        out_specs=(vmem,) * 5,
        scratch_shapes=[pltpu.VMEM(shape, kind) for shape, kind in shapes]
        + [pltpu.SemaphoreType.DMA((count,)), pltpu.SemaphoreType.DMA((count,)), pltpu.SemaphoreType.DMA((2,))],
        compiler_params=pltpu.CompilerParams(
            collective_id=0, has_side_effects=True, vmem_limit_bytes=56 * 1024 * 1024),
        name="window_block",
    )(image, cotangent, gain.reshape(1, features), w_qkv, w_out, table)


def add_kernel(img_ref, cot_ref, att_ref, gtok_ref, gqkv_in, gout_in, ggain_in,
               out_ref, gimg_ref, gqkv_ref, gout_ref, ggain_ref):
    f32, bf16 = jnp.float32, jnp.bfloat16
    out_ref[...] = (img_ref[...].astype(f32) + att_ref[...].astype(f32)).astype(bf16)
    gimg_ref[...] = (cot_ref[...].astype(f32) + gtok_ref[...].astype(f32)).astype(bf16)
    gqkv_ref[...] = gqkv_in[...]
    gout_ref[...] = gout_in[...]
    ggain_ref[...] = ggain_in[...]


def add_branches(image, cotangent, attention, grad_tokens, grad_qkv, grad_out, grad_gain):
    rows, cols, features = image.shape
    steps = 2
    tile = pl.BlockSpec((rows // steps, cols, features), lambda i: (i, 0, 0))
    small = [pl.BlockSpec(value.shape, lambda i: (0, 0)) for value in (grad_qkv, grad_out, grad_gain)]
    return pl.pallas_call(
        add_kernel,
        grid=(steps,),
        out_shape=(
            jax.ShapeDtypeStruct(image.shape, image.dtype), jax.ShapeDtypeStruct(image.shape, image.dtype),
            jax.ShapeDtypeStruct(grad_qkv.shape, jnp.float32), jax.ShapeDtypeStruct(grad_out.shape, jnp.float32),
            jax.ShapeDtypeStruct(grad_gain.shape, jnp.float32),
        ),
        in_specs=[tile] * 4 + small,
        out_specs=(tile, tile, *small),
        name="add_branches",
    )(image, cotangent, attention, grad_tokens, grad_qkv, grad_out, grad_gain)


def local(image, cotangent, gain, w_qkv, w_out, bias_table):
    total_count = (
        lax.axis_size("rows")
        * lax.axis_size("cols")
        * lax.axis_size("rep")
        * image.shape[1]
        * image.shape[2]
    )
    factor = 1.0 / float(np.sqrt(total_count))
    branches = block(
        image[0], cotangent[0], gain, w_qkv, w_out, bias_table,
        lax.axis_size("rows") // 2, lax.axis_size("rep"), factor)
    result, grad_result, grad_qkv, grad_out, grad_gain = add_branches(image[0], cotangent[0], *branches)
    return (result[None], grad_result[None], grad_qkv, grad_out.T, grad_gain.reshape(4))


def solution(mesh):
    in_specs = (P("rep", "rows", "cols", None), P("rep", "rows", "cols", None), P(), P(), P(), P())
    out_specs = (
        P("rep", "rows", "cols", None),
        P("rep", "rows", "cols", None),
        P(("rows", "cols", "rep"), None),
        P(None, ("rows", "cols", "rep")),
        P(("rows", "cols", "rep")),
    )
    return jax.shard_map(local, mesh=mesh, in_specs=in_specs, out_specs=out_specs, check_vma=False)
```

```python
import functools

import jax
import jax.numpy as jnp
import numpy as np
from jax import lax
from jax.experimental import pallas as pl
from jax.experimental.pallas import tpu as pltpu
from jax.sharding import PartitionSpec as P

MESH = pl.DeviceIdType.MESH
EPS = 1e-06
GROUP = 256
HEAD = 64
PARTS = (("yxz", 0, 0), ("xyz", 0, 512), ("yxz", 1, 0), ("xyz", 1, 512))


def token_place(index):
    return (index // 32) * 4 + (index % 16) // 4, ((index // 16) % 2) * 4 + index % 4


def nt(left, right):
    return lax.dot_general(left, right, (((1,), (1,)), ((), ())), preferred_element_type=jnp.float32)


def tn(left, right):
    return lax.dot_general(left, right, (((0,), (0,)), ((), ())), preferred_element_type=jnp.float32)


def nn(left, right):
    return jnp.dot(left, right, preferred_element_type=jnp.float32)


def block_place(rb, cb):
    if cb == 0:
        return ("corner", 0, 0) if rb == 3 else ("left", rb, 0)
    if rb in (1, 2):
        return ("window", 3, (rb - 1) * 2) if cb == 7 else ("window", (cb - 1) // 2, (rb - 1) * 2 + (cb - 1) % 2)
    if rb == 3:
        return ("window", 4 + (cb - 1) // 2, (cb - 1) % 2) if cb <= 4 else ("down", cb - 5, 0)
    if cb <= 4:
        return ("up", (cb - 1) // 2, (cb - 1) % 2)
    return ("window", 7, 2) if cb == 7 else ("window", 6, 2 + cb - 5)


def kernel(nz, nx, factor,
           img_ref, cot_ref, gain_ref, wqkv_hbm, wout_hbm, table3_ref,
           att_ref, gtok_ref, gqkv_ref, gout_ref, ggain_ref,
           wqkv_ref, wout_ref, tok, ret,
           up, down, left, corner, b_up, b_down, b_left, b_corner,
           norm_t, g_t, inv_ref, proj, gheads, heads, gproj, bias_ref, table_ref,
           m_ref, recv0, *rest):
    f32, bf16, i32 = jnp.float32, jnp.bfloat16, jnp.int32
    count_parts = len(PARTS)
    acc1, acc2, acc3 = rest[0:4], rest[4:8], rest[8:12]
    rx1, rx2, rx3 = rest[12:16], rest[16:20], rest[20:24]
    sends, recvs, local_sems = rest[24:]
    scale = HEAD ** -0.5
    all_heads = 2 * GROUP

    row, col, x = lax.axis_index("rows"), lax.axis_index("cols"), lax.axis_index("rep")
    yh, z = row // nz, row % nz
    yl, core = col // 2, col % 2
    y = yh * 2 + yl
    place = {"x": x, "y": y, "z": z}
    size = {"x": nx, "y": 4, "z": nz}
    pair = (row, yl * 2 + 1 - core, x)
    above = ((row + 2 * nz - 1) % (2 * nz), col, x)
    below = ((row + 1) % (2 * nz), col, x)
    lefty = (row, (col + 3) % 4, x)
    right = (row, (col + 1) % 4, x)
    below_left = ((row + 1) % (2 * nz), (col + 3) % 4, x)
    above_right = ((row + 2 * nz - 1) % (2 * nz), (col + 1) % 4, x)

    def on(axis, step):
        other = (place[axis] + step) % size[axis]
        if axis == "x":
            return other, (row, col, other)
        if axis == "y":
            return other, ((other // 2) * nz + z, (other % 2) * 2 + core, x)
        return other, (yh * nz + other, col, x)

    copies = [
        pltpu.make_async_copy(wqkv_hbm, wqkv_ref, local_sems.at[0]),
        pltpu.make_async_copy(wout_hbm, wout_ref, local_sems.at[1]),
    ]
    for copy in copies:
        copy.start()

    barrier = pltpu.get_barrier_semaphore()
    peers = [pair, above, below, lefty, right, below_left, above_right]
    for axis in "xyz":
        peers += [on(axis, step)[1] for step in range(1, size[axis])]
    for peer in peers:
        pl.semaphore_signal(barrier, inc=1, device_id=peer, device_id_type=MESH)

    slot = iter(range(1000))
    started = []

    def send(source, target, device):
        index = next(slot)
        copy = pltpu.make_async_remote_copy(
            src_ref=source, dst_ref=target, send_sem=sends.at[index], recv_sem=recvs.at[index],
            device_id=device, device_id_type=MESH)
        copy.start()
        started.append(copy)
        return copy

    def landed(arrivals):
        for copy in arrivals:
            copy.wait_recv()

    rim = {"up": up, "down": down, "left": left, "corner": corner}
    back = {"up": b_up, "down": b_down, "left": b_left, "corner": b_corner}
    one = lax.broadcasted_iota(i32, (128, 128), 0)
    two = lax.broadcasted_iota(i32, (128, 128), 1)
    to_block = (two == ((one % 16) // 4) * 32 + (one // 16) * 4 + one % 4).astype(bf16)
    from_block = (two == ((one % 32) // 4) * 16 + (one // 32) * 4 + one % 4).astype(bf16)

    def block_at(own, rims, which, spot):
        name, a, b = spot
        if name == "window":
            return own.at[which, a, b]
        return rims[name].at[which, a, b]

    for rb in (0, 3, 1, 2):
        for which, ref in ((0, img_ref), (1, cot_ref)):
            value = nn(to_block, ref[rb * 4:rb * 4 + 4].reshape(128, 1024)).astype(bf16)
            for cb in range(8):
                block_at(tok, rim, which, block_place(rb, cb))[...] = value[cb * 16:cb * 16 + 16]

    pl.semaphore_wait(barrier, len(peers))
    from_right = [
        send(left.at[:, 1, 0], tok.at[:, 3, 1], lefty),
        send(left.at[:, 2, 0], tok.at[:, 3, 3], lefty),
    ]
    from_below = [send(up, tok.at[:, 4:6, 2:4], above)]
    from_above = [
        send(down.at[:, 0, 0], tok.at[:, 6, 0], below),
        send(down.at[:, 1, 0], tok.at[:, 6, 1], below),
        send(down.at[:, 2, 0], tok.at[:, 7, 0], below),
        send(corner.at[:, 0, 0], tok.at[:, 7, 1], below_left),
        send(left.at[:, 0, 0], tok.at[:, 7, 3], lefty),
    ]

    krow, kcol = token_place(lax.broadcasted_iota(i32, (64, 128), 0))
    qrow, qcol = token_place(lax.broadcasted_iota(i32, (64, 128), 1) % 64)
    offset = (qrow - krow + 7) * 16 + qcol - kcol + 7
    low, low_half = offset % 128, offset < 128
    first_head = lax.broadcasted_iota(i32, (64, 128), 1) < 64

    for dr in range(15):
        table_ref[:, dr * 16:dr * 16 + 15] = table3_ref[dr]

    def bias_of(head):
        at = functools.partial(jnp.take_along_axis, indices=low, axis=1, mode="promise_in_bounds")
        one_half = at(jnp.broadcast_to(table_ref[head:head + 1, 0:128], (64, 128)))
        return jnp.where(low_half, one_half, at(jnp.broadcast_to(table_ref[head:head + 1, 128:256], (64, 128))))

    for duo in range(4):
        bias_ref[duo // 2, :, (duo % 2) * 128:(duo % 2) * 128 + 128] = jnp.where(
            first_head, bias_of(2 * duo), bias_of(2 * duo + 1))

    def chunk(step):
        return slice(step * 128, step * 128 + 128)

    def project(step):
        part = chunk(step)
        value = tok[0, 2 * step:2 * step + 2].reshape(128, 1024).astype(f32)
        inverse = lax.rsqrt(jnp.mean(value * value, axis=1, keepdims=True) + EPS)
        inv_ref[part, :] = inverse
        normed = (value * inverse * gain_ref[...]).astype(bf16)
        upstream = tok[1, 2 * step:2 * step + 2].reshape(128, 1024)
        norm_t[step] = normed.T
        g_t[step] = upstream.T
        proj[part, :] = nn(normed, wqkv_ref[...]).astype(bf16)
        gheads[part, :] = nt(upstream, wout_ref[...]).astype(bf16)

    head_row = lax.broadcasted_iota(i32, (GROUP, GROUP), 0) // HEAD
    head_lane = lax.broadcasted_iota(i32, (GROUP, GROUP), 1) // HEAD
    diagonal = head_row == head_lane
    lane64 = lax.broadcasted_iota(i32, (64, GROUP), 1) // HEAD

    def spread(value):
        return jnp.where(diagonal, jnp.concatenate([value] * 4, axis=0), jnp.zeros((), value.dtype))

    def gather_heads(full):
        out = full[0:64]
        for h in range(1, 4):
            out = jnp.where(lane64 == h, full[h * 64:h * 64 + 64], out)
        return out

    def attend(win, grp):
        part = pl.ds(pl.multiple_of(win * 64, 64), 64)
        lo = grp * GROUP
        cq = slice(lo, lo + GROUP)
        ck = slice(all_heads + lo, all_heads + lo + GROUP)
        cv = slice(2 * all_heads + lo, 2 * all_heads + lo + GROUP)
        q, k, v, go = proj[part, cq], proj[part, ck], proj[part, cv], gheads[part, cq]
        q_wide, go_wide = spread(q), spread(go)
        scores = nt(k, q_wide) * scale + bias_ref[grp]
        expo = jnp.exp(scores - jnp.max(scores, axis=0, keepdims=True))
        soft = expo * (1.0 / jnp.sum(expo, axis=0, keepdims=True))
        soft_b = soft.astype(bf16)
        gp = nt(v, go_wide)
        inner = jnp.sum(gp * soft, axis=0, keepdims=True)
        gs = (soft * (gp - inner) * scale).astype(bf16)
        heads[part, cq] = gather_heads(tn(soft_b, v)).astype(bf16)
        gproj[part, cq] = gather_heads(tn(gs, k)).astype(bf16)
        gproj[part, ck] = nn(gs, q_wide).astype(bf16)
        gproj[part, cv] = nn(soft_b, go_wide).astype(bf16)

    def attend_range(first, last, grp):
        def body(win, carry):
            attend(win, grp)
            return carry

        lax.fori_loop(first, last, body, 0)

    def weights(grp, half):
        lo = grp * GROUP

        def body(step, carry):
            rows = pl.ds(pl.multiple_of(half * 512 + step * 128, 128), 128)
            from_norm = jnp.concatenate([norm_t[t, rows, :] for t in range(4)], axis=1)
            from_g = jnp.concatenate([g_t[t, rows, :] for t in range(4)], axis=1)
            zs = pl.ds(step * 2, 2)
            for kind in range(3):
                cols = slice(kind * all_heads + lo, kind * all_heads + lo + GROUP)
                value = nn(from_norm, gproj[:, cols]).astype(bf16)
                m_ref[grp, half, zs, :, :, :, kind * GROUP:kind * GROUP + GROUP] = value.reshape(2, 2, 2, 16, GROUP)
            value = nn(from_g, heads[:, lo:lo + GROUP]).astype(bf16)
            m_ref[grp, half, zs, :, :, :, 3 * GROUP:] = value.reshape(2, 2, 2, 16, GROUP)
            return carry

        lax.fori_loop(0, nz // 2, body, 0)
        return send(m_ref.at[grp, half, :, :, 1 - core], recv0.at[grp, half], pair)

    def exchange(source, target, axis):
        return [send(source.at[on(axis, s)[0]], target.at[s - 1], on(axis, s)[1]) for s in range(1, size[axis])]

    def pair_add(index):
        order, grp, lo = PARTS[index]

        def body(block, carry):
            a, b, c = block // (2 * nz), (block // 2) % nz, block % 2
            cols = slice(lo, lo + 512)
            value = m_ref[grp, a, b, c, core, :, cols].astype(f32) + recv0[grp, a, b, c, :, cols].astype(f32)
            for part in range(nx):
                rows = value[part * 4:part * 4 + 4]
                tile = jnp.concatenate([rows[:, j * 128:j * 128 + 128] for j in range(4)], axis=0)
                at = {"x": part, "y": a * 2 + c, "z": b}
                acc1[index][at[order[0]], at[order[1]], at[order[2]]] = tile.astype(bf16)
            return carry

        lax.fori_loop(0, 4 * nz, body, 0, unroll=4)
        return exchange(acc1[index], rx1[index], order[0])

    def sum_one(index, arrivals):
        order = PARTS[index][0]
        landed(arrivals)
        mine = place[order[0]]

        def body(j, carry):
            for k in range(size[order[2]]):
                value = acc1[index][mine, j, k].astype(f32)
                for s in range(size[order[0]] - 1):
                    value = value + rx1[index][s, j, k].astype(f32)
                acc2[index][j, k] = value.astype(bf16)
            return carry

        lax.fori_loop(0, size[order[1]], body, 0)
        return exchange(acc2[index], rx2[index], order[1])

    def sum_two(index, arrivals):
        order = PARTS[index][0]
        landed(arrivals)
        mine = place[order[1]]
        for k in range(size[order[2]]):
            value = acc2[index][mine, k].astype(f32)
            for s in range(size[order[1]] - 1):
                value = value + rx2[index][s, k].astype(f32)
            acc3[index][k] = value.astype(bf16)
        return exchange(acc3[index], rx3[index], order[2])

    def sum_three(index, arrivals):
        order = PARTS[index][0]
        landed(arrivals)
        value = acc3[index][place[order[2]]].astype(f32)
        for s in range(size[order[2]] - 1):
            value = value + rx3[index][s].astype(f32)
        return value

    def finish(step):
        part = chunk(step)
        att = nn(heads[part, :], wout_ref[...]).astype(bf16)
        grad_normed = nt(gproj[part, :], wqkv_ref[...])
        inverse = inv_ref[part, :]
        unit = tok[0, 2 * step:2 * step + 2].reshape(128, 1024).astype(f32) * inverse
        grad_unit = grad_normed * gain_ref[...]
        mean = jnp.mean(grad_unit * unit, axis=1, keepdims=True)
        ret[0, 2 * step:2 * step + 2] = att.reshape(2, 4, 16, 1024)
        ret[1, 2 * step:2 * step + 2] = (inverse * (grad_unit - unit * mean)).astype(bf16).reshape(2, 4, 16, 1024)

    def residual(rb):
        for which, target in ((0, att_ref), (1, gtok_ref)):
            value = jnp.concatenate(
                [block_at(ret, back, which, block_place(rb, cb))[...] for cb in range(8)], axis=0)
            target[rb * 4:rb * 4 + 4] = nn(from_block, value).astype(bf16).reshape(4, 32, 1024)

    for copy in copies:
        copy.wait()
    project(0)
    attend_range(0, 2, 0)
    landed(from_right)
    project(1)
    attend_range(2, 4, 0)
    attend_range(0, 4, 1)
    landed(from_below)
    project(2)
    attend_range(4, 6, 0)
    landed(from_above)
    project(3)
    attend_range(6, 8, 0)
    paired0 = [weights(0, 0), weights(0, 1)]
    attend_range(4, 6, 1)
    landed(paired0)
    p0 = pair_add(0)
    p1 = pair_add(1)
    attend_range(6, 8, 1)
    paired1 = [weights(1, 0), weights(1, 1)]
    finish(2)
    landed(paired1)
    p2 = pair_add(2)
    p3 = pair_add(3)
    finish(3)
    p0 = sum_one(0, p0)
    p1 = sum_one(1, p1)
    finish(1)
    finish(0)
    p0 = sum_two(0, p0)
    p1 = sum_two(1, p1)
    p2 = sum_one(2, p2)
    p3 = sum_one(3, p3)
    b_above = [send(ret.at[:, 4:6, 2:4], b_up, below)]
    b_below = [
        send(ret.at[:, 6, 0], b_down.at[:, 0, 0], above),
        send(ret.at[:, 6, 1], b_down.at[:, 1, 0], above),
        send(ret.at[:, 7, 0], b_down.at[:, 2, 0], above),
    ]
    b_lefty = [
        send(ret.at[:, 7, 1], b_corner.at[:, 0, 0], above_right),
        send(ret.at[:, 7, 3], b_left.at[:, 0, 0], right),
    ]
    b_lefty += [
        send(ret.at[:, 3, 1], b_left.at[:, 1, 0], right),
        send(ret.at[:, 3, 3], b_left.at[:, 2, 0], right),
    ]
    p2 = sum_two(2, p2)
    p3 = sum_two(3, p3)
    landed(b_lefty)
    residual(1)
    residual(2)
    landed(b_above)
    residual(0)
    landed(b_below)
    residual(3)
    arrivals = [p0, p1, p2, p3]
    for index in range(count_parts):
        grp, lo = PARTS[index][1:]
        got = sum_three(index, arrivals[index]) * factor
        for j in range(4):
            kind, within = divmod(lo + j * 128, GROUP)
            start = grp * GROUP + within
            if kind < 3:
                start += kind * all_heads
                gqkv_ref[:, start:start + 128] = got[j * 4:j * 4 + 4]
            else:
                gout_ref[:, start:start + 128] = got[j * 4:j * 4 + 4]
    block = yh * (4 * nz) + z * 4 + yl * 2 + core
    own_rows = wqkv_ref[pl.ds(pl.multiple_of(block * 16, 16), 16), :].astype(f32)
    own = own_rows[0:4]
    for other in range(1, nx):
        own = jnp.where(x == other, own_rows[other * 4:other * 4 + 4], own)
    lane = lax.broadcasted_iota(i32, (4, 1024), 1)
    mine = lane == (block * nx + x) * 4 + lax.broadcasted_iota(i32, (4, 1024), 0)
    own_gain = jnp.sum(jnp.where(mine, gain_ref[...], 0.0), axis=1, keepdims=True)
    value = jnp.sum(own * gqkv_ref[...], axis=1, keepdims=True) / own_gain
    spot = lax.broadcasted_iota(i32, (4, 128), 0) == lax.broadcasted_iota(i32, (4, 128), 1)
    ggain_ref[...] = jnp.sum(jnp.where(spot, value, 0.0), axis=0, keepdims=True)[:, 0:4]
    for copy in started:
        copy.wait_send()


def block(image, cotangent, gain, w_qkv, w_out, bias_table, nz, nx, factor):
    f32, bf16 = jnp.float32, jnp.bfloat16
    features = image.shape[-1]
    table = bias_table.transpose(1, 0, 2)
    size = {"x": nx, "y": 4, "z": nz}
    wide = 128
    orders = [part[0] for part in PARTS]
    dims = [[size[axis] for axis in order] for order in orders]
    shapes = [
        (w_qkv.shape, bf16), (w_out.shape, bf16),
        ((2, 8, 4, 16, features), bf16), ((2, 8, 4, 16, features), bf16),
    ]
    for _ in range(2):
        shapes += [((2, 2, 2, 16, features), bf16), ((2, 3, 1, 16, features), bf16),
                   ((2, 3, 1, 16, features), bf16), ((2, 1, 1, 16, features), bf16)]
    shapes += [
        ((4, features, 128), bf16), ((4, features, 128), bf16), ((512, 1), f32),
        ((512, 1536), bf16), ((512, 512), bf16), ((512, 512), bf16), ((512, 1536), bf16), ((2, 64, 256), f32), ((8, 256), f32),
        ((2, 2, nz, 2, 2, 16, 1024), bf16), ((2, 2, nz, 2, 16, 1024), bf16),
    ]
    shapes += [((a, b, c, 16, wide), bf16) for a, b, c in dims]
    shapes += [((b, c, 16, wide), bf16) for a, b, c in dims]
    shapes += [((c, 16, wide), bf16) for a, b, c in dims]
    shapes += [((a - 1, b, c, 16, wide), bf16) for a, b, c in dims]
    shapes += [((b - 1, c, 16, wide), bf16) for a, b, c in dims]
    shapes += [((c - 1, 16, wide), bf16) for a, b, c in dims]
    count = 8 + 4 + 8 + len(PARTS) * (nx + nz + 4 - 3)
    vmem, hbm = pl.BlockSpec(memory_space=pltpu.VMEM), pl.BlockSpec(memory_space=pl.ANY)
    return pl.pallas_call(
        functools.partial(kernel, nz, nx, factor),
        out_shape=(
            jax.ShapeDtypeStruct(image.shape, bf16), jax.ShapeDtypeStruct(image.shape, bf16),
            jax.ShapeDtypeStruct((4, 1536), f32), jax.ShapeDtypeStruct((4, 512), f32),
            jax.ShapeDtypeStruct((1, 4), f32),
        ),
        in_specs=[vmem, vmem, vmem, hbm, hbm, vmem],
        out_specs=(vmem,) * 5,
        scratch_shapes=[pltpu.VMEM(shape, kind) for shape, kind in shapes]
        + [pltpu.SemaphoreType.DMA((count,)), pltpu.SemaphoreType.DMA((count,)), pltpu.SemaphoreType.DMA((2,))],
        compiler_params=pltpu.CompilerParams(
            collective_id=0, has_side_effects=True, vmem_limit_bytes=56 * 1024 * 1024),
        name="window_block",
    )(image, cotangent, gain.reshape(1, features), w_qkv, w_out, table)


def add_kernel(img_ref, cot_ref, att_ref, gtok_ref, gqkv_in, gout_in, ggain_in,
               out_ref, gimg_ref, gqkv_ref, gout_ref, ggain_ref):
    f32, bf16 = jnp.float32, jnp.bfloat16
    out_ref[...] = (img_ref[...].astype(f32) + att_ref[...].astype(f32)).astype(bf16)
    gimg_ref[...] = (cot_ref[...].astype(f32) + gtok_ref[...].astype(f32)).astype(bf16)
    gqkv_ref[...] = gqkv_in[...]
    gout_ref[...] = gout_in[...]
    ggain_ref[...] = ggain_in[...]


def add_branches(image, cotangent, attention, grad_tokens, grad_qkv, grad_out, grad_gain):
    rows, cols, features = image.shape
    steps = 2
    tile = pl.BlockSpec((rows // steps, cols, features), lambda i: (i, 0, 0))
    small = [pl.BlockSpec(value.shape, lambda i: (0, 0)) for value in (grad_qkv, grad_out, grad_gain)]
    return pl.pallas_call(
        add_kernel,
        grid=(steps,),
        out_shape=(
            jax.ShapeDtypeStruct(image.shape, image.dtype), jax.ShapeDtypeStruct(image.shape, image.dtype),
            jax.ShapeDtypeStruct(grad_qkv.shape, jnp.float32), jax.ShapeDtypeStruct(grad_out.shape, jnp.float32),
            jax.ShapeDtypeStruct(grad_gain.shape, jnp.float32),
        ),
        in_specs=[tile] * 4 + small,
        out_specs=(tile, tile, *small),
        name="add_branches",
    )(image, cotangent, attention, grad_tokens, grad_qkv, grad_out, grad_gain)


def local(image, cotangent, gain, w_qkv, w_out, bias_table):
    total_count = (
        lax.axis_size("rows")
        * lax.axis_size("cols")
        * lax.axis_size("rep")
        * image.shape[1]
        * image.shape[2]
    )
    factor = 1.0 / float(np.sqrt(total_count))
    branches = block(
        image[0], cotangent[0], gain, w_qkv, w_out, bias_table,
        lax.axis_size("rows") // 2, lax.axis_size("rep"), factor)
    result, grad_result, grad_qkv, grad_out, grad_gain = add_branches(image[0], cotangent[0], *branches)
    return (result[None], grad_result[None], grad_qkv, grad_out.T, grad_gain.reshape(4))


def solution(mesh):
    in_specs = (P("rep", "rows", "cols", None), P("rep", "rows", "cols", None), P(), P(), P(), P())
    out_specs = (
        P("rep", "rows", "cols", None),
        P("rep", "rows", "cols", None),
        P(("rows", "cols", "rep"), None),
        P(None, ("rows", "cols", "rep")),
        P(("rows", "cols", "rep")),
    )
    return jax.shard_map(local, mesh=mesh, in_specs=in_specs, out_specs=out_specs, check_vma=False)
```
